32 devices in a mesh: view: 2 (over core), sky: 16 (over z, y, x).
Axes of the slice: x: 2, y: 2, z: 4, core: 2. Of those that a mesh axis runs over, the one named last changes fastest.
Arguments:
- pixels: bfloat16 [2, 32768, 128], P('view', 'sky'), may hold values from -6 to 6
- cotangent: bfloat16 [2, 32768, 128], P('view', 'sky'), may hold values from -6 to 6
- filters: bfloat16 [4, 128, 128], replicated, may hold values from -0.25 to 0.25
- lap_tiles: bfloat16 [16, 24, 256, 256], P('sky'), may hold values from -0.15625 to 0.15625
- tile_target: int32 [16, 24], P('sky'), may hold values from 0 to 7
- tile_source: int32 [16, 24], P('sky'), may hold values from 0 to 15
- tile_count: int32 [16], P('sky'), may hold values from 12 to 24, as said below
- send_blocks: int32 [16, 4, 2], P('sky'), may hold values from 0 to 7
Outputs:
- outputs: bfloat16 [2, 32768, 128], P('view', 'sky')
- pixel_grad: bfloat16 [2, 32768, 128], P('view', 'sky')
- filter_grad: float32 [4, 128, 128], replicated
The draws below stay inside these ranges and needn't reach their ends.
Inputs may be any that keep to these rules, and one draw needn't show every extreme that they name: `tile_count`: every device has at least half of 24 live tiles, and some device has exactly 24. `tile_source`: indices below 8 are own blocks, the others received ones.
All inputs are finite; a program needn't handle non-finite values.
Results may differ from the reference program's by a relative error of at most 0.017.
Values may be sent and summed in bfloat16 or wider, within the bound.
A program may use at most 64 MiB of HBM per device.

```python
import math
import jax
import jax.numpy as jnp
from jax import lax

C = 128
BLK = 256
K = 4
NB = 8
NSEND = 2
MAXT = 24
NEXT = 16
SKY_DEVS = 16
VIEWS = 2
NPIX = 32768


def draw_tile_count(key, part):
    counts = jax.random.randint(key, (SKY_DEVS,), MAXT // 2, MAXT + 1)
    chosen = jax.random.randint(jax.random.fold_in(key, 7), (), 0, SKY_DEVS)
    return counts.at[chosen].set(MAXT).astype(jnp.int32)


def with_ends(values, rng, least, top_value):
    longest = values.shape.index(max(values.shape))
    spots = []
    for shift in (0, 1):
        where = [jax.random.randint(jax.random.fold_in(rng, axis), (), 0, length) for axis, length in enumerate(values.shape)]
        where[longest] = (where[longest] + shift) % values.shape[longest]
        spots.append(tuple(where))
    return values.at[spots[0]].set(least).at[spots[1]].set(top_value)


def block_scale(stream_key, extent, cuts, least, largest):
    loudness = 1.0
    for axis_at, parts in cuts:
        steps = jax.random.uniform(jax.random.fold_in(jax.random.fold_in(stream_key, 6), axis_at), (parts,), jnp.float32, least / len(cuts), largest / len(cuts))
        loudness = loudness * jnp.repeat(jnp.exp(steps), extent[axis_at] // parts).reshape((-1,) + (1,) * (len(extent) - 1 - axis_at))
    return loudness


def bell_draw(key, shape, deviation, most, cuts=(), kind=jnp.bfloat16):
    factor_of = block_scale(key, shape, cuts, -0.22, 0.18) if cuts else 1.0
    entries = jax.random.normal(key, shape, jnp.float32) * deviation * factor_of
    return jnp.minimum(jnp.maximum(entries, -most), most).astype(kind)


def setup_inputs(seed: int = 0) -> dict:
    keys = jax.random.split(jax.random.key(seed), 9)
    return {
        "pixels": bell_draw(keys[0], (VIEWS, NPIX, C), 1.0, 6.0, ((0, 2), (1, 16))),
        "cotangent": bell_draw(keys[1], (VIEWS, NPIX, C), 1.0, 6.0, ((0, 2), (1, 16))),
        "filters": bell_draw(keys[2], (K, C, C), (K * C) ** -0.5, 0.25),
        "lap_tiles": bell_draw(keys[3], (SKY_DEVS, MAXT, BLK, BLK), (6 * BLK) ** -0.5, 0.15625, ((0, 16),)),
        "tile_target": with_ends(jax.random.randint(keys[4], (SKY_DEVS, MAXT), 0, NB), jax.random.fold_in(keys[4], 1), 0, NB - 1).astype(jnp.int32),
        "tile_source": with_ends(jax.random.randint(keys[5], (SKY_DEVS, MAXT), 0, NEXT), jax.random.fold_in(keys[5], 1), 0, NEXT - 1).astype(jnp.int32),
        "tile_count": draw_tile_count(jax.random.fold_in(keys[8], 71), 0),
        "send_blocks": with_ends(jax.random.randint(keys[7], (SKY_DEVS, 4, NSEND), 0, NB), jax.random.fold_in(keys[7], 1), 0, NB - 1).astype(jnp.int32),
    }


OFFSETS = (1, -1, 2, -2)

def shifted(values, offset):
    filler = jnp.zeros((abs(offset),) + values.shape[1:], values.dtype)
    if offset > 0:
        return jnp.concatenate([filler, values[:-offset]], axis=0)
    return jnp.concatenate([values[-offset:], filler], axis=0)

def extend(blocks, send_blocks):
    pieces = [blocks]
    for number, offset in enumerate(OFFSETS):
        picked = jax.vmap(lambda source, chosen: source[chosen])(blocks, send_blocks[:, number])
        pieces.append(shifted(picked, offset))
    return jnp.concatenate(pieces, axis=1)

def forward_pass(blocks, lap_tiles, tile_target, tile_source, tile_count, send_blocks):
    extended = extend(blocks, send_blocks)

    def one_device(operands):
        tile_set, target, source, live_count, ext_blocks = operands
        gathered = ext_blocks[source].astype(jnp.float32)
        products = jnp.einsum('tpq,tqc->tpc', tile_set.astype(jnp.float32), gathered)
        live_mask = jnp.arange(MAXT) < live_count
        routing = ((target[None, :] == jnp.arange(NB)[:, None]) & live_mask[None, :]).astype(jnp.float32)
        return jnp.einsum('bt,tpc->bpc', routing, products)
    return lax.map(one_device, (lap_tiles, tile_target, tile_source, tile_count, extended))

def transposed_pass(blocks, lap_tiles, tile_target, tile_source, tile_count, send_blocks):

    def one_device(operands):
        tile_set, target, source, live_count, own_blocks = operands
        picked = own_blocks[target].astype(jnp.float32)
        products = jnp.einsum('tpq,tpc->tqc', tile_set.astype(jnp.float32), picked)
        live_mask = jnp.arange(MAXT) < live_count
        routing = ((source[None, :] == jnp.arange(NEXT)[:, None]) & live_mask[None, :]).astype(jnp.float32)
        return jnp.einsum('et,tqc->eqc', routing, products)
    slot_sums = lax.map(one_device, (lap_tiles, tile_target, tile_source, tile_count, blocks))
    combined = slot_sums[:, :NB]
    for number, offset in enumerate(OFFSETS):
        begin = NB + number * NSEND
        back = shifted(slot_sums[:, begin:begin + NSEND], -offset)
        routing = (send_blocks[:, number, None, :] == jnp.arange(NB)[None, :, None]).astype(jnp.float32)
        combined = combined + jnp.einsum('dbj,djqc->dbqc', routing, back)
    return combined

def reference(pixels, cotangent, filters, lap_tiles, tile_target, tile_source, tile_count, send_blocks):
    graph = (lap_tiles, tile_target, tile_source, tile_count, send_blocks)
    outputs = []
    adjoints = []
    filter_sum = jnp.zeros((K, C, C), jnp.float32)
    for view in range(VIEWS):
        base = pixels[view].reshape(SKY_DEVS, NB, BLK, C)
        cheb_one = forward_pass(base, *graph).astype(jnp.bfloat16)
        cheb_two = (2.0 * forward_pass(cheb_one, *graph) - base.astype(jnp.float32)).astype(jnp.bfloat16)
        cheb_three = (2.0 * forward_pass(cheb_two, *graph) - cheb_one.astype(jnp.float32)).astype(jnp.bfloat16)
        flattened = [member.reshape(NPIX, C) for member in (base, cheb_one, cheb_two, cheb_three)]
        result = jnp.dot(flattened[0], filters[0], preferred_element_type=jnp.float32)
        for order in range(1, K):
            result = result + jnp.dot(flattened[order], filters[order], preferred_element_type=jnp.float32)
        outputs.append(result.astype(jnp.bfloat16))
        upstream = cotangent[view]
        pulled = [jnp.dot(upstream, filters[order].T, preferred_element_type=jnp.float32).reshape(SKY_DEVS, NB, BLK, C) for order in range(K)]
        adj_three = pulled[3]
        adj_two = pulled[2] + 2.0 * transposed_pass(adj_three.astype(jnp.bfloat16), *graph)
        adj_one = pulled[1] + 2.0 * transposed_pass(adj_two.astype(jnp.bfloat16), *graph) - adj_three
        adj_zero = pulled[0] + transposed_pass(adj_one.astype(jnp.bfloat16), *graph) - adj_two
        adjoints.append(adj_zero.reshape(NPIX, C).astype(jnp.bfloat16))
        filter_sum = filter_sum + jnp.stack([jnp.dot(flattened[order].T, upstream, preferred_element_type=jnp.float32) for order in range(K)])
    scale = 1.0 / math.sqrt(VIEWS * NPIX)
    return (jnp.stack(outputs), jnp.stack(adjoints), filter_sum * scale)
```

```python
import functools
import math

import jax
import jax.numpy as jnp
from jax import lax
from jax.experimental import pallas as pl
from jax.experimental.pallas import tpu as pltpu
from jax.sharding import PartitionSpec as P

OFFSETS = (1, -1, 2, -2)
MESH = pl.DeviceIdType.MESH
STRIDE = 64
BIG = 1 << 20
GROUP = 8


def radices_of(size):
    found = []
    while size > 1:
        step = 4 if size % 4 == 0 else (2 if size % 2 == 0 else size)
        found.append(step)
        size //= step
    return found


def smallest(values):
    while len(values) > 1:
        paired = [jnp.minimum(a, b) for a, b in zip(values[::2], values[1::2])]
        values = paired + (values[-1:] if len(values) % 2 else [])
    return values[0]


def order_slots(keys, key_count, perm, keep, last):
    codes = [key * STRIDE + number for number, key in enumerate(keys)]

    def pick(place, carry):
        before, before_key = carry
        code = smallest([jnp.where(c > before, c, BIG) for c in codes])
        key = lax.div(code, STRIDE)
        perm[place] = code - key * STRIDE
        keep[place] = jnp.where(key == before_key, 1.0, 0.0).astype(jnp.float32)
        return code, key

    lax.fori_loop(0, len(keys), pick, (jnp.int32(-1), jnp.int32(-1)))

    def ends(key, carry):
        upto = sum(jnp.where(c < (key + 1) * STRIDE, 1, 0) for c in codes)
        under = sum(jnp.where(c < key * STRIDE, 1, 0) for c in codes)
        last[key] = jnp.where(upto > under, upto, 0)
        return carry

    lax.fori_loop(0, key_count, ends, 0)


def kernel(
    sky_size, scale,
    pixels, cotangent, filters, target, source, live, chosen, tiles_hbm,
    outputs, pixel_grad, filter_grad,
    tiles, ext0, ext1, ext2, latest, out_f0, out_f1, out_f2, out_b0, out_b1, out_b2,
    in_b0, in_b1, in_b2, cot_t, u, adj_three, adj_two, adj_one, adj_zero,
    part_f, part_b, part_a, grads,
    red_send_a, red_land_a, red_out_a, red_slots_a, red_final_a,
    red_send_b, red_land_b, red_out_b, red_slots_b, red_final_b,
    perm_f, perm_b, perm_a, keep_f, keep_b, keep_a, last_f, last_b, last_a,
    tile_sem, f_send, f_recv, b_send, b_recv, r_send, r_recv,
):
    me = lax.axis_index("sky")
    view = lax.axis_index("view")
    blocks, size, channels = pixels.shape
    max_tiles = tiles.shape[0]
    ext_count = ext0.shape[0]
    sends = (ext_count - blocks) // len(OFFSETS)
    radices = radices_of(sky_size)
    exts, outs_f = (ext0, ext1, ext2), (out_f0, out_f1, out_f2)
    outs_b, ins_b = (out_b0, out_b1, out_b2), (in_b0, in_b1, in_b2)

    tile_copy = pltpu.make_async_copy(tiles_hbm, tiles, tile_sem)
    tile_copy.start()

    def inside(place):
        return jnp.logical_and(place >= 0, place < sky_size)

    groups = []
    below = 1
    for radix in radices:
        spot = lax.rem(lax.div(me, below), radix)
        groups.append((below, radix, spot))
        below *= radix

    def partner(group, shift):
        below, radix, spot = group
        return me + (lax.rem(spot + shift, radix) - spot) * below

    barrier = pltpu.get_barrier_semaphore()
    peers = 1
    for offset in OFFSETS:
        peers = peers + jnp.where(inside(me + offset), 1, 0)
        @pl.when(inside(me + offset))
        def _():
            pl.semaphore_signal(barrier, inc=1, device_id={"sky": me + offset}, device_id_type=MESH)
    for group in groups:
        for shift in range(1, group[1]):
            other = partner(group, shift)
            far = (other - me) * (other - me) > 4
            peers = peers + jnp.where(far, 1, 0)
            @pl.when(far)
            def _():
                pl.semaphore_signal(barrier, inc=1, device_id={"sky": other}, device_id_type=MESH)
    pl.semaphore_signal(barrier, inc=1, device_id={"view": 1 - view}, device_id_type=MESH)

    for number, offset in enumerate(OFFSETS):
        at = pl.ds(blocks + number * sends, sends)
        @pl.when(jnp.logical_not(inside(me - offset)))
        def _():
            for ext in exts:
                ext[at] = jnp.zeros((sends, size, channels), jnp.bfloat16)

        @pl.when(jnp.logical_not(inside(me + offset)))
        def _():
            for landed in ins_b:
                landed[pl.ds(number * sends, sends)] = jnp.zeros(
                    (sends, channels, size), jnp.bfloat16
                )

    def stage_forward(step, blocks_ref):
        for slot in range(len(OFFSETS) * sends):
            outs_f[step][slot] = blocks_ref[chosen[slot]]

    def copy_forward(step, number):
        return pltpu.make_async_remote_copy(
            src_ref=outs_f[step].at[pl.ds(number * sends, sends)],
            dst_ref=exts[step].at[pl.ds(blocks + number * sends, sends)],
            send_sem=f_send.at[step, number],
            recv_sem=f_recv.at[step, number],
            device_id={"sky": me + OFFSETS[number]},
            device_id_type=MESH,
        )

    def copy_backward(step, number):
        return pltpu.make_async_remote_copy(
            src_ref=outs_b[step].at[pl.ds(number * sends, sends)],
            dst_ref=ins_b[step].at[pl.ds(number * sends, sends)],
            send_sem=b_send.at[step, number],
            recv_sem=b_recv.at[step, number],
            device_id={"sky": me - OFFSETS[number]},
            device_id_type=MESH,
        )

    def start_all(copy, step, sign):
        for number in (3, 2, 1, 0):
            @pl.when(inside(me + sign * OFFSETS[number]))
            def _():
                copy(step, number).start()

    def wait_arrivals(copy, step, sign):
        for number in range(len(OFFSETS)):
            @pl.when(inside(me - sign * OFFSETS[number]))
            def _():
                copy(step, number).wait_recv()

    def wait_departures(copy, step, sign):
        for number in range(len(OFFSETS)):
            @pl.when(inside(me + sign * OFFSETS[number]))
            def _():
                copy(step, number).wait_send()

    stage_forward(0, pixels)
    pl.semaphore_wait(barrier, peers)
    start_all(copy_forward, 0, 1)

    ext0[pl.ds(0, blocks)] = pixels[...]
    part_f[0] = jnp.zeros(part_f.shape[1:], jnp.float32)
    part_b[0] = jnp.zeros(part_b.shape[1:], jnp.float32)
    part_a[0] = jnp.zeros(part_a.shape[1:], jnp.float32)
    count = live[0]
    live_target = [jnp.where(t < count, target[t], blocks) for t in range(max_tiles)]
    live_source = [jnp.where(t < count, source[t], ext_count) for t in range(max_tiles)]
    order_slots(live_source, ext_count, perm_b, keep_b, last_b)
    order_slots([chosen[t] for t in range(len(OFFSETS) * sends)], blocks, perm_a, keep_a, last_a)
    order_slots(live_target, blocks, perm_f, keep_f, last_f)

    for b in range(blocks):
        cot_t[:, b * size : (b + 1) * size] = (
            cotangent[b].astype(jnp.float32).T.astype(jnp.bfloat16)
        )

    group = GROUP if max_tiles % GROUP == 0 else 1

    def scan_tiles(product, perm, keep, part):
        def body(step, total):
            for inner in range(group):
                place = step * group + inner
                total = product(perm[place]) + keep[place] * total
                part[place + 1] = total
            return total

        lax.fori_loop(0, max_tiles // group, body, jnp.zeros(part.shape[1:], jnp.float32))

    def forward(step):
        def product(t):
            return jnp.dot(
                tiles[t], exts[step][source[t]], preferred_element_type=jnp.float32
            )

        scan_tiles(product, perm_f, keep_f, part_f)

    def transposed(step):
        def product(t):
            return jnp.dot(u[target[t]], tiles[t], preferred_element_type=jnp.float32)

        scan_tiles(product, perm_b, keep_b, part_b)
        for slot in range(ext_count - blocks):
            outs_b[step][slot] = part_b[last_b[blocks + slot]].astype(jnp.bfloat16)
        start_all(copy_backward, step, -1)

    def add_arrivals(step):
        wait_arrivals(copy_backward, step, -1)
        total = jnp.zeros((channels, size), jnp.float32)
        for place in range(len(OFFSETS) * sends):
            total = ins_b[step][perm_a[place]].astype(jnp.float32) + keep_a[place] * total
            part_a[place + 1] = total

    def pulled(order, b):
        return jnp.dot(
            filters[order], cot_t[:, b * size : (b + 1) * size],
            preferred_element_type=jnp.float32,
        )

    def gradient(order, member):
        found = jnp.dot(
            cot_t[...], member.reshape(blocks * size, channels),
            preferred_element_type=jnp.float32,
        )
        grads[pl.ds(order * channels, channels)] = found

    reducers = (
        (0, 3, red_send_a, red_land_a, red_out_a, red_slots_a, red_final_a),
        (3, 4, red_send_b, red_land_b, red_out_b, red_slots_b, red_final_b),
    )
    per_batch = 2 + sum(radix - 1 for radix in radices)

    def half_of(batch):
        return (reducers[batch][1] - reducers[batch][0]) * channels // 2

    def view_copy(batch, src, dst, sem):
        return pltpu.make_async_remote_copy(
            src_ref=src, dst_ref=dst,
            send_sem=r_send.at[batch, sem], recv_sem=r_recv.at[batch, sem],
            device_id={"view": 1 - view}, device_id_type=MESH,
        )

    def halves_copy(batch):
        return view_copy(batch, reducers[batch][2], reducers[batch][3], 0)

    def final_copy(batch):
        half = half_of(batch)
        mine = reducers[batch][6].at[pl.ds(pl.multiple_of(view * half, 16), half)]
        return view_copy(batch, mine, mine, 1)

    def group_copy(batch, level, shift):
        sem = 2 + sum(radix - 1 for radix in radices[:level]) + shift - 1
        return pltpu.make_async_remote_copy(
            src_ref=reducers[batch][4].at[level],
            dst_ref=reducers[batch][5].at[level, groups[level][2]],
            send_sem=r_send.at[batch, sem], recv_sem=r_recv.at[batch, sem],
            device_id={"sky": partner(groups[level], shift)}, device_id_type=MESH,
        )

    def send_halves(batch):
        first, half = reducers[batch][0] * channels, half_of(batch)
        theirs = pl.multiple_of(first + (1 - view) * half, 16)
        reducers[batch][2][...] = grads[pl.ds(theirs, half)].astype(jnp.bfloat16)
        halves_copy(batch).start()

    def send_level(batch, level, total):
        rounded = total.astype(jnp.bfloat16)
        reducers[batch][4][level] = rounded
        reducers[batch][5][level, groups[level][2]] = rounded
        for shift in range(1, radices[level]):
            group_copy(batch, level, shift).start()

    def sum_level(batch, level):
        for shift in range(1, radices[level]):
            group_copy(batch, level, shift).wait_recv()
        total = reducers[batch][5][level, 0].astype(jnp.float32)
        for spot in range(1, radices[level]):
            total = total + reducers[batch][5][level, spot].astype(jnp.float32)
        return total

    def reduce_step(batch, step):
        if step == 0:
            send_halves(batch)
            return
        if step == 1:
            halves_copy(batch).wait_recv()
            first, half = reducers[batch][0] * channels, half_of(batch)
            mine = pl.multiple_of(first + view * half, 16)
            total = grads[pl.ds(mine, half)] + reducers[batch][3][...].astype(jnp.float32)
        elif step <= 1 + len(radices):
            total = sum_level(batch, step - 2)
        else:
            final_copy(batch).wait_recv()
            for order in range(reducers[batch][0], reducers[batch][1]):
                at = pl.ds((order - reducers[batch][0]) * channels, channels)
                filter_grad[order] = (reducers[batch][6][at] * scale).T
            return
        if step <= len(radices):
            send_level(batch, step - 1, total)
        else:
            half = half_of(batch)
            reducers[batch][6][pl.ds(pl.multiple_of(view * half, 16), half)] = total
            final_copy(batch).start()

    steps = 3 + len(radices)

    for b in range(blocks):
        value = pulled(3, b)
        adj_three[b] = value
        u[b] = value.astype(jnp.bfloat16)
    tile_copy.wait()
    transposed(0)
    for b in range(blocks):
        adj_two[b] = pulled(2, b) + 2.0 * part_b[last_b[b]]

    wait_arrivals(copy_forward, 0, 1)
    forward(0)
    for b in range(blocks):
        value = part_f[last_f[b]].astype(jnp.bfloat16)
        ext1[b] = value
        latest[b] = value
    stage_forward(1, latest)
    start_all(copy_forward, 1, 1)
    gradient(0, pixels[...])
    gradient(1, ext1[pl.ds(0, blocks)])

    add_arrivals(0)
    for b in range(blocks):
        value = adj_two[b] + 2.0 * part_a[last_a[b]]
        adj_two[b] = value
        u[b] = value.astype(jnp.bfloat16)
    transposed(1)
    for b in range(blocks):
        adj_one[b] = pulled(1, b) + 2.0 * part_b[last_b[b]] - adj_three[b]

    wait_arrivals(copy_forward, 1, 1)
    forward(1)
    for b in range(blocks):
        value = 2.0 * part_f[last_f[b]] - pixels[b].astype(jnp.float32)
        ext2[b] = value.astype(jnp.bfloat16)
        latest[b] = value.astype(jnp.bfloat16)
    stage_forward(2, latest)
    start_all(copy_forward, 2, 1)
    gradient(2, ext2[pl.ds(0, blocks)])
    reduce_step(0, 0)

    add_arrivals(1)
    for b in range(blocks):
        value = adj_one[b] + 2.0 * part_a[last_a[b]]
        adj_one[b] = value
        u[b] = value.astype(jnp.bfloat16)
    transposed(2)
    reduce_step(0, 1)
    for b in range(blocks):
        adj_zero[b] = pulled(0, b) + part_b[last_b[b]] - adj_two[b]

    wait_arrivals(copy_forward, 2, 1)
    forward(2)
    for b in range(blocks):
        value = 2.0 * part_f[last_f[b]] - ext1[b].astype(jnp.float32)
        latest[b] = value.astype(jnp.bfloat16)
    gradient(3, latest[...])
    reduce_step(1, 0)
    reduce_step(0, 2)
    reduce_step(1, 1)

    weights = filters[...].reshape(filters.shape[0] * channels, channels)
    for b in range(blocks):
        joined = jnp.concatenate([pixels[b], ext1[b], ext2[b], latest[b]], axis=1)
        outputs[b] = jnp.dot(joined, weights, preferred_element_type=jnp.float32).astype(
            jnp.bfloat16
        )
    for step in range(2, steps):
        if step > 2:
            reduce_step(0, step)
        reduce_step(1, step)

    add_arrivals(2)
    for b in range(blocks):
        value = adj_zero[b] + part_a[last_a[b]]
        pixel_grad[b] = value.T.astype(jnp.bfloat16)

    for step in range(3):
        wait_departures(copy_forward, step, 1)
        wait_departures(copy_backward, step, -1)
    for batch in range(2):
        halves_copy(batch).wait_send()
        for level in range(len(radices)):
            for shift in range(1, radices[level]):
                group_copy(batch, level, shift).wait_send()
        final_copy(batch).wait_send()


def per_device(
    sky_size, view_size,
    pixels, cotangent, filters, lap_tiles, tile_target, tile_source, tile_count, send_blocks
):
    _, max_tiles, size, _ = lap_tiles.shape
    rows, channels = pixels.shape[1:]
    orders = filters.shape[0]
    blocks = rows // size
    slots = send_blocks.shape[1] * send_blocks.shape[2]
    ext_count = blocks + slots
    radices = radices_of(sky_size)
    bf, f32 = jnp.bfloat16, jnp.float32
    vmem = functools.partial(pl.BlockSpec, memory_space=pltpu.VMEM)
    smem = functools.partial(pl.BlockSpec, memory_space=pltpu.SMEM)

    def reducer(count):
        half = count * channels // 2
        return [
            pltpu.VMEM((half, channels), bf),
            pltpu.VMEM((half, channels), bf),
            pltpu.VMEM((len(radices), half, channels), bf),
            pltpu.VMEM((len(radices), max(radices), half, channels), bf),
            pltpu.VMEM((2 * half, channels), f32),
        ]

    sems = 2 + sum(radix - 1 for radix in radices)
    scratch = (
        [pltpu.VMEM((max_tiles, size, size), bf)]
        + [pltpu.VMEM((ext_count, size, channels), bf)] * 3
        + [pltpu.VMEM((blocks, size, channels), bf)]
        + [pltpu.VMEM((slots, size, channels), bf)] * 3
        + [pltpu.VMEM((slots, channels, size), bf)] * 6
        + [pltpu.VMEM((channels, rows), bf), pltpu.VMEM((blocks, channels, size), bf)]
        + [pltpu.VMEM((blocks, channels, size), f32)] * 4
        + [
            pltpu.VMEM((max_tiles + 1, size, channels), f32),
            pltpu.VMEM((max_tiles + 1, channels, size), f32),
            pltpu.VMEM((slots + 1, channels, size), f32),
            pltpu.VMEM((orders * channels, channels), f32),
        ]
        + reducer(3)
        + reducer(1)
        + [pltpu.SMEM((max_tiles,), jnp.int32)] * 2
        + [pltpu.SMEM((slots,), jnp.int32)]
        + [pltpu.SMEM((max_tiles,), f32)] * 2
        + [pltpu.SMEM((slots,), f32)]
        + [
            pltpu.SMEM((blocks,), jnp.int32),
            pltpu.SMEM((ext_count,), jnp.int32),
            pltpu.SMEM((blocks,), jnp.int32),
        ]
        + [pltpu.SemaphoreType.DMA]
        + [pltpu.SemaphoreType.DMA((3, len(OFFSETS)))] * 4
        + [pltpu.SemaphoreType.DMA((2, sems))] * 2
    )
    scale = 1.0 / math.sqrt(view_size * sky_size * rows)
    flops = 2 * channels * (6 * max_tiles * size * size + 3 * orders * rows * channels)
    outputs, pixel_grad, filter_grad = pl.pallas_call(
        functools.partial(kernel, sky_size, scale),
        out_shape=(
            jax.ShapeDtypeStruct((blocks, size, channels), bf),
            jax.ShapeDtypeStruct((blocks, size, channels), bf),
            jax.ShapeDtypeStruct((orders, channels, channels), f32),
        ),
        in_specs=[vmem()] * 3 + [smem()] * 4 + [pl.BlockSpec(memory_space=pl.ANY)],
        out_specs=(vmem(),) * 3,
        scratch_shapes=scratch,
        cost_estimate=pl.CostEstimate(
            flops=flops, bytes_accessed=2 * max_tiles * size * size, transcendentals=0
        ),
        compiler_params=pltpu.CompilerParams(
            collective_id=0, has_side_effects=True, vmem_limit_bytes=48 * 1024 * 1024
        ),
    )(
        pixels.reshape(blocks, size, channels),
        cotangent.reshape(blocks, size, channels),
        filters,
        tile_target.reshape(max_tiles),
        tile_source.reshape(max_tiles),
        tile_count,
        send_blocks.reshape(slots),
        lap_tiles.reshape(max_tiles, size, size),
    )
    return (
        outputs.reshape(1, rows, channels),
        pixel_grad.reshape(1, rows, channels),
        filter_grad,
    )


def solution(mesh):
    return jax.shard_map(
        functools.partial(per_device, mesh.shape["sky"], mesh.shape["view"]),
        mesh=mesh,
        in_specs=(
            P("view", "sky", None),
            P("view", "sky", None),
            P(),
            P("sky", None, None, None),
            P("sky", None),
            P("sky", None),
            P("sky"),
            P("sky", None, None),
        ),
        out_specs=(P("view", "sky", None), P("view", "sky", None), P()),
        check_vma=False,
    )
```

```python
import functools
import math

import jax
import jax.numpy as jnp
from jax import lax
from jax.experimental import pallas as pl
from jax.experimental.pallas import tpu as pltpu
from jax.sharding import PartitionSpec as P

OFFSETS = (1, -1, 2, -2)
MESH = pl.DeviceIdType.MESH
STRIDE = 64
BIG = 1 << 20
GROUP = 8


def radices_of(size):
    found = []
    while size > 1:
        step = 4 if size % 4 == 0 else (2 if size % 2 == 0 else size)
        found.append(step)
        size //= step
    return found


def smallest(values):
    while len(values) > 1:
        paired = [jnp.minimum(a, b) for a, b in zip(values[::2], values[1::2])]
        values = paired + (values[-1:] if len(values) % 2 else [])
    return values[0]


def order_slots(keys, key_count, perm, keep, last):
    codes = [key * STRIDE + number for number, key in enumerate(keys)]

    def pick(place, carry):
        before, before_key = carry
        code = smallest([jnp.where(c > before, c, BIG) for c in codes])
        key = lax.div(code, STRIDE)
        perm[place] = code - key * STRIDE
        keep[place] = jnp.where(key == before_key, 1.0, 0.0).astype(jnp.float32)
        return code, key

    lax.fori_loop(0, len(keys), pick, (jnp.int32(-1), jnp.int32(-1)))

    def ends(key, carry):
        upto = sum(jnp.where(c < (key + 1) * STRIDE, 1, 0) for c in codes)
        under = sum(jnp.where(c < key * STRIDE, 1, 0) for c in codes)
        last[key] = jnp.where(upto > under, upto, 0)
        return carry

    lax.fori_loop(0, key_count, ends, 0)


def kernel(
    sky_size, scale,
    pixels_in, cotangent_in, filters_in, target, source, live, chosen, tiles_in,
    outputs_out, pixel_grad_out, filter_grad_out,
    pixels, cotangent, filters, outputs, pixel_grad, filter_grad,
    tiles, ext0, ext1, ext2, latest, out_f0, out_f1, out_f2, out_b0, out_b1, out_b2,
    in_b0, in_b1, in_b2, cot_t, u, adj_three, adj_two, adj_one, adj_zero,
    part_f, part_b, part_a, grads,
    red_send_a, red_land_a, red_out_a, red_slots_a, red_final_a,
    red_send_b, red_land_b, red_out_b, red_slots_b, red_final_b,
    perm_f, perm_b, perm_a, keep_f, keep_b, keep_a, last_f, last_b, last_a,
    in_sem, out_sem, f_send, f_recv, b_send, b_recv, r_send, r_recv,
):
    me = lax.axis_index("sky")
    view = lax.axis_index("view")
    blocks, size, channels = pixels.shape
    max_tiles = tiles.shape[0]
    ext_count = ext0.shape[0]
    sends = (ext_count - blocks) // len(OFFSETS)
    radices = radices_of(sky_size)
    exts, outs_f = (ext0, ext1, ext2), (out_f0, out_f1, out_f2)
    outs_b, ins_b = (out_b0, out_b1, out_b2), (in_b0, in_b1, in_b2)

    loads = [
        pltpu.make_async_copy(src, dst, in_sem.at[number])
        for number, (src, dst) in enumerate((
            (pixels_in, pixels),
            (cotangent_in, cotangent),
            (filters_in, filters),
            (pixels_in, ext0.at[pl.ds(0, blocks)]),
            (tiles_in, tiles),
        ))
    ]
    stores = [
        pltpu.make_async_copy(src, dst, out_sem.at[number])
        for number, (src, dst) in enumerate((
            (outputs, outputs_out), (filter_grad, filter_grad_out), (pixel_grad, pixel_grad_out)
        ))
    ]
    for load in loads:
        load.start()

    def inside(place):
        return jnp.logical_and(place >= 0, place < sky_size)

    groups = []
    below = 1
    for radix in radices:
        spot = lax.rem(lax.div(me, below), radix)
        groups.append((below, radix, spot))
        below *= radix

    def partner(group, shift):
        below, radix, spot = group
        return me + (lax.rem(spot + shift, radix) - spot) * below

    barrier = pltpu.get_barrier_semaphore()
    peers = 1
    for offset in OFFSETS:
        peers = peers + jnp.where(inside(me + offset), 1, 0)
        @pl.when(inside(me + offset))
        def _():
            pl.semaphore_signal(barrier, inc=1, device_id={"sky": me + offset}, device_id_type=MESH)
    for group in groups:
        for shift in range(1, group[1]):
            other = partner(group, shift)
            far = (other - me) * (other - me) > 4
            peers = peers + jnp.where(far, 1, 0)
            @pl.when(far)
            def _():
                pl.semaphore_signal(barrier, inc=1, device_id={"sky": other}, device_id_type=MESH)
    pl.semaphore_signal(barrier, inc=1, device_id={"view": 1 - view}, device_id_type=MESH)

    for number, offset in enumerate(OFFSETS):
        at = pl.ds(blocks + number * sends, sends)
        @pl.when(jnp.logical_not(inside(me - offset)))
        def _():
            for ext in exts:
                ext[at] = jnp.zeros((sends, size, channels), jnp.bfloat16)

        @pl.when(jnp.logical_not(inside(me + offset)))
        def _():
            for landed in ins_b:
                landed[pl.ds(number * sends, sends)] = jnp.zeros(
                    (sends, channels, size), jnp.bfloat16
                )

    def stage_forward(step, blocks_ref):
        for slot in range(len(OFFSETS) * sends):
            outs_f[step][slot] = blocks_ref[chosen[slot]]

    def copy_forward(step, number):
        return pltpu.make_async_remote_copy(
            src_ref=outs_f[step].at[pl.ds(number * sends, sends)],
            dst_ref=exts[step].at[pl.ds(blocks + number * sends, sends)],
            send_sem=f_send.at[step, number],
            recv_sem=f_recv.at[step, number],
            device_id={"sky": me + OFFSETS[number]},
            device_id_type=MESH,
        )

    def copy_backward(step, number):
        return pltpu.make_async_remote_copy(
            src_ref=outs_b[step].at[pl.ds(number * sends, sends)],
            dst_ref=ins_b[step].at[pl.ds(number * sends, sends)],
            send_sem=b_send.at[step, number],
            recv_sem=b_recv.at[step, number],
            device_id={"sky": me - OFFSETS[number]},
            device_id_type=MESH,
        )

    def start_all(copy, step, sign):
        for number in (3, 2, 1, 0):
            @pl.when(inside(me + sign * OFFSETS[number]))
            def _():
                copy(step, number).start()

    def wait_arrivals(copy, step, sign):
        for number in range(len(OFFSETS)):
            @pl.when(inside(me - sign * OFFSETS[number]))
            def _():
                copy(step, number).wait_recv()

    def wait_departures(copy, step, sign):
        for number in range(len(OFFSETS)):
            @pl.when(inside(me + sign * OFFSETS[number]))
            def _():
                copy(step, number).wait_send()

    loads[0].wait()
    stage_forward(0, pixels)
    pl.semaphore_wait(barrier, peers)
    start_all(copy_forward, 0, 1)

    part_f[0] = jnp.zeros(part_f.shape[1:], jnp.float32)
    part_b[0] = jnp.zeros(part_b.shape[1:], jnp.float32)
    part_a[0] = jnp.zeros(part_a.shape[1:], jnp.float32)
    count = live[0]
    live_target = [jnp.where(t < count, target[t], blocks) for t in range(max_tiles)]
    live_source = [jnp.where(t < count, source[t], ext_count) for t in range(max_tiles)]
    order_slots(live_source, ext_count, perm_b, keep_b, last_b)
    order_slots([chosen[t] for t in range(len(OFFSETS) * sends)], blocks, perm_a, keep_a, last_a)
    order_slots(live_target, blocks, perm_f, keep_f, last_f)

    loads[1].wait()
    for b in range(blocks):
        cot_t[:, b * size : (b + 1) * size] = (
            cotangent[b].astype(jnp.float32).T.astype(jnp.bfloat16)
        )

    group = GROUP if max_tiles % GROUP == 0 else 1

    def scan_tiles(product, perm, keep, part):
        def body(step, total):
            for inner in range(group):
                place = step * group + inner
                total = product(perm[place]) + keep[place] * total
                part[place + 1] = total
            return total

        lax.fori_loop(0, max_tiles // group, body, jnp.zeros(part.shape[1:], jnp.float32))

    def forward(step):
        def product(t):
            return jnp.dot(
                tiles[t], exts[step][source[t]], preferred_element_type=jnp.float32
            )

        scan_tiles(product, perm_f, keep_f, part_f)

    def transposed(step):
        def product(t):
            return jnp.dot(u[target[t]], tiles[t], preferred_element_type=jnp.float32)

        scan_tiles(product, perm_b, keep_b, part_b)
        for slot in range(ext_count - blocks):
            outs_b[step][slot] = part_b[last_b[blocks + slot]].astype(jnp.bfloat16)
        start_all(copy_backward, step, -1)

    def add_arrivals(step):
        wait_arrivals(copy_backward, step, -1)
        total = jnp.zeros((channels, size), jnp.float32)
        for place in range(len(OFFSETS) * sends):
            total = ins_b[step][perm_a[place]].astype(jnp.float32) + keep_a[place] * total
            part_a[place + 1] = total

    def pulled(order, b):
        return jnp.dot(
            filters[order], cot_t[:, b * size : (b + 1) * size],
            preferred_element_type=jnp.float32,
        )

    def gradient(order, member):
        found = jnp.dot(
            cot_t[...], member.reshape(blocks * size, channels),
            preferred_element_type=jnp.float32,
        )
        grads[pl.ds(order * channels, channels)] = found

    reducers = (
        (0, 3, red_send_a, red_land_a, red_out_a, red_slots_a, red_final_a),
        (3, 4, red_send_b, red_land_b, red_out_b, red_slots_b, red_final_b),
    )
    per_batch = 2 + sum(radix - 1 for radix in radices)

    def half_of(batch):
        return (reducers[batch][1] - reducers[batch][0]) * channels // 2

    def view_copy(batch, src, dst, sem):
        return pltpu.make_async_remote_copy(
            src_ref=src, dst_ref=dst,
            send_sem=r_send.at[batch, sem], recv_sem=r_recv.at[batch, sem],
            device_id={"view": 1 - view}, device_id_type=MESH,
        )

    def halves_copy(batch):
        return view_copy(batch, reducers[batch][2], reducers[batch][3], 0)

    def final_copy(batch):
        half = half_of(batch)
        mine = reducers[batch][6].at[pl.ds(pl.multiple_of(view * half, 16), half)]
        return view_copy(batch, mine, mine, 1)

    def group_copy(batch, level, shift):
        sem = 2 + sum(radix - 1 for radix in radices[:level]) + shift - 1
        return pltpu.make_async_remote_copy(
            src_ref=reducers[batch][4].at[level],
            dst_ref=reducers[batch][5].at[level, groups[level][2]],
            send_sem=r_send.at[batch, sem], recv_sem=r_recv.at[batch, sem],
            device_id={"sky": partner(groups[level], shift)}, device_id_type=MESH,
        )

    def send_halves(batch):
        first, half = reducers[batch][0] * channels, half_of(batch)
        theirs = pl.multiple_of(first + (1 - view) * half, 16)
        reducers[batch][2][...] = grads[pl.ds(theirs, half)].astype(jnp.bfloat16)
        halves_copy(batch).start()

    def send_level(batch, level, total):
        rounded = total.astype(jnp.bfloat16)
        reducers[batch][4][level] = rounded
        reducers[batch][5][level, groups[level][2]] = rounded
        for shift in range(1, radices[level]):
            group_copy(batch, level, shift).start()

    def sum_level(batch, level):
        for shift in range(1, radices[level]):
            group_copy(batch, level, shift).wait_recv()
        total = reducers[batch][5][level, 0].astype(jnp.float32)
        for spot in range(1, radices[level]):
            total = total + reducers[batch][5][level, spot].astype(jnp.float32)
        return total

    def reduce_step(batch, step):
        if step == 0:
            send_halves(batch)
            return
        if step == 1:
            halves_copy(batch).wait_recv()
            first, half = reducers[batch][0] * channels, half_of(batch)
            mine = pl.multiple_of(first + view * half, 16)
            total = grads[pl.ds(mine, half)] + reducers[batch][3][...].astype(jnp.float32)
        elif step <= 1 + len(radices):
            total = sum_level(batch, step - 2)
        else:
            final_copy(batch).wait_recv()
            for order in range(reducers[batch][0], reducers[batch][1]):
                at = pl.ds((order - reducers[batch][0]) * channels, channels)
                filter_grad[order] = (reducers[batch][6][at] * scale).T
            return
        if step <= len(radices):
            send_level(batch, step - 1, total)
        else:
            half = half_of(batch)
            reducers[batch][6][pl.ds(pl.multiple_of(view * half, 16), half)] = total
            final_copy(batch).start()

    steps = 3 + len(radices)

    loads[2].wait()
    for b in range(blocks):
        value = pulled(3, b)
        adj_three[b] = value
        u[b] = value.astype(jnp.bfloat16)
    loads[4].wait()
    transposed(0)
    for b in range(blocks):
        adj_two[b] = pulled(2, b) + 2.0 * part_b[last_b[b]]

    loads[3].wait()
    wait_arrivals(copy_forward, 0, 1)
    forward(0)
    for b in range(blocks):
        value = part_f[last_f[b]].astype(jnp.bfloat16)
        ext1[b] = value
        latest[b] = value
    stage_forward(1, latest)
    start_all(copy_forward, 1, 1)
    gradient(0, pixels[...])
    gradient(1, ext1[pl.ds(0, blocks)])

    add_arrivals(0)
    for b in range(blocks):
        value = adj_two[b] + 2.0 * part_a[last_a[b]]
        adj_two[b] = value
        u[b] = value.astype(jnp.bfloat16)
    transposed(1)
    for b in range(blocks):
        adj_one[b] = pulled(1, b) + 2.0 * part_b[last_b[b]] - adj_three[b]

    wait_arrivals(copy_forward, 1, 1)
    forward(1)
    for b in range(blocks):
        value = 2.0 * part_f[last_f[b]] - pixels[b].astype(jnp.float32)
        ext2[b] = value.astype(jnp.bfloat16)
        latest[b] = value.astype(jnp.bfloat16)
    stage_forward(2, latest)
    start_all(copy_forward, 2, 1)
    gradient(2, ext2[pl.ds(0, blocks)])
    reduce_step(0, 0)

    add_arrivals(1)
    for b in range(blocks):
        value = adj_one[b] + 2.0 * part_a[last_a[b]]
        adj_one[b] = value
        u[b] = value.astype(jnp.bfloat16)
    transposed(2)
    reduce_step(0, 1)
    for b in range(blocks):
        adj_zero[b] = pulled(0, b) + part_b[last_b[b]] - adj_two[b]

    wait_arrivals(copy_forward, 2, 1)
    forward(2)
    for b in range(blocks):
        value = 2.0 * part_f[last_f[b]] - ext1[b].astype(jnp.float32)
        latest[b] = value.astype(jnp.bfloat16)
    gradient(3, latest[...])
    reduce_step(1, 0)
    reduce_step(0, 2)
    reduce_step(1, 1)

    weights = filters[...].reshape(filters.shape[0] * channels, channels)
    for b in range(blocks):
        joined = jnp.concatenate([pixels[b], ext1[b], ext2[b], latest[b]], axis=1)
        outputs[b] = jnp.dot(joined, weights, preferred_element_type=jnp.float32).astype(
            jnp.bfloat16
        )
    stores[0].start()
    for step in range(2, steps):
        if step > 2:
            reduce_step(0, step)
        reduce_step(1, step)
    stores[1].start()

    add_arrivals(2)
    for b in range(blocks):
        value = adj_zero[b] + part_a[last_a[b]]
        pixel_grad[b] = value.T.astype(jnp.bfloat16)
    stores[2].start()

    for step in range(3):
        wait_departures(copy_forward, step, 1)
        wait_departures(copy_backward, step, -1)
    for batch in range(2):
        halves_copy(batch).wait_send()
        for level in range(len(radices)):
            for shift in range(1, radices[level]):
                group_copy(batch, level, shift).wait_send()
        final_copy(batch).wait_send()
    for store in stores:
        store.wait()


def per_device(
    sky_size, view_size,
    pixels, cotangent, filters, lap_tiles, tile_target, tile_source, tile_count, send_blocks
):
    _, max_tiles, size, _ = lap_tiles.shape
    rows, channels = pixels.shape[1:]
    orders = filters.shape[0]
    blocks = rows // size
    slots = send_blocks.shape[1] * send_blocks.shape[2]
    ext_count = blocks + slots
    radices = radices_of(sky_size)
    bf, f32 = jnp.bfloat16, jnp.float32
    anywhere = pl.BlockSpec(memory_space=pl.ANY)
    smem = functools.partial(pl.BlockSpec, memory_space=pltpu.SMEM)

    def reducer(count):
        half = count * channels // 2
        return [
            pltpu.VMEM((half, channels), bf),
            pltpu.VMEM((half, channels), bf),
            pltpu.VMEM((len(radices), half, channels), bf),
            pltpu.VMEM((len(radices), max(radices), half, channels), bf),
            pltpu.VMEM((2 * half, channels), f32),
        ]

    sems = 2 + sum(radix - 1 for radix in radices)
    scratch = (
        [pltpu.VMEM((blocks, size, channels), bf)] * 2
        + [pltpu.VMEM((orders, channels, channels), bf)]
        + [pltpu.VMEM((blocks, size, channels), bf)] * 2
        + [pltpu.VMEM((orders, channels, channels), f32)]
        + [pltpu.VMEM((max_tiles, size, size), bf)]
        + [pltpu.VMEM((ext_count, size, channels), bf)] * 3
        + [pltpu.VMEM((blocks, size, channels), bf)]
        + [pltpu.VMEM((slots, size, channels), bf)] * 3
        + [pltpu.VMEM((slots, channels, size), bf)] * 6
        + [pltpu.VMEM((channels, rows), bf), pltpu.VMEM((blocks, channels, size), bf)]
        + [pltpu.VMEM((blocks, channels, size), f32)] * 4
        + [
            pltpu.VMEM((max_tiles + 1, size, channels), f32),
            pltpu.VMEM((max_tiles + 1, channels, size), f32),
            pltpu.VMEM((slots + 1, channels, size), f32),
            pltpu.VMEM((orders * channels, channels), f32),
        ]
        + reducer(3)
        + reducer(1)
        + [pltpu.SMEM((max_tiles,), jnp.int32)] * 2
        + [pltpu.SMEM((slots,), jnp.int32)]
        + [pltpu.SMEM((max_tiles,), f32)] * 2
        + [pltpu.SMEM((slots,), f32)]
        + [
            pltpu.SMEM((blocks,), jnp.int32),
            pltpu.SMEM((ext_count,), jnp.int32),
            pltpu.SMEM((blocks,), jnp.int32),
        ]
        + [pltpu.SemaphoreType.DMA((5,)), pltpu.SemaphoreType.DMA((3,))]
        + [pltpu.SemaphoreType.DMA((3, len(OFFSETS)))] * 4
        + [pltpu.SemaphoreType.DMA((2, sems))] * 2
    )
    scale = 1.0 / math.sqrt(view_size * sky_size * rows)
    flops = 2 * channels * (6 * max_tiles * size * size + 3 * orders * rows * channels)
    outputs, pixel_grad, filter_grad = pl.pallas_call(
        functools.partial(kernel, sky_size, scale),
        out_shape=(
            jax.ShapeDtypeStruct((blocks, size, channels), bf),
            jax.ShapeDtypeStruct((blocks, size, channels), bf),
            jax.ShapeDtypeStruct((orders, channels, channels), f32),
        ),
        in_specs=[anywhere] * 3 + [smem()] * 4 + [anywhere],
        out_specs=(anywhere,) * 3,
        scratch_shapes=scratch,
        cost_estimate=pl.CostEstimate(
            flops=flops, bytes_accessed=2 * max_tiles * size * size, transcendentals=0
        ),
        compiler_params=pltpu.CompilerParams(
            collective_id=0, has_side_effects=True, vmem_limit_bytes=60 * 1024 * 1024
        ),
    )(
        pixels.reshape(blocks, size, channels),
        cotangent.reshape(blocks, size, channels),
        filters,
        tile_target.reshape(max_tiles),
        tile_source.reshape(max_tiles),
        tile_count,
        send_blocks.reshape(slots),
        lap_tiles.reshape(max_tiles, size, size),
    )
    return (
        outputs.reshape(1, rows, channels),
        pixel_grad.reshape(1, rows, channels),
        filter_grad,
    )


def solution(mesh):
    return jax.shard_map(
        functools.partial(per_device, mesh.shape["sky"], mesh.shape["view"]),
        mesh=mesh,
        in_specs=(
            P("view", "sky", None),
            P("view", "sky", None),
            P(),
            P("sky", None, None, None),
            P("sky", None),
            P("sky", None),
            P("sky"),
            P("sky", None, None),
        ),
        out_specs=(P("view", "sky", None), P("view", "sky", None), P()),
        check_vma=False,
    )
```

```python
import functools
import math

import jax
import jax.numpy as jnp
from jax import lax
from jax.experimental import pallas as pl
from jax.experimental.pallas import tpu as pltpu
from jax.sharding import PartitionSpec as P

OFFSETS = (1, -1, 2, -2)
MESH = pl.DeviceIdType.MESH
STRIDE = 64
BIG = 1 << 20
GROUP = 8


def radices_of(size):
    found = []
    while size > 1:
        step = 4 if size % 4 == 0 else (2 if size % 2 == 0 else size)
        found.append(step)
        size //= step
    return found


def smallest(values):
    while len(values) > 1:
        paired = [jnp.minimum(a, b) for a, b in zip(values[::2], values[1::2])]
        values = paired + (values[-1:] if len(values) % 2 else [])
    return values[0]


def order_slots(keys, key_count, perm, keep, last):
    codes = [key * STRIDE + number for number, key in enumerate(keys)]

    def pick(place, carry):
        before, before_key = carry
        code = smallest([jnp.where(c > before, c, BIG) for c in codes])
        key = lax.div(code, STRIDE)
        perm[place] = code - key * STRIDE
        keep[place] = jnp.where(key == before_key, 1.0, 0.0).astype(jnp.float32)
        return code, key

    lax.fori_loop(0, len(keys), pick, (jnp.int32(-1), jnp.int32(-1)))

    def ends(key, carry):
        upto = sum(jnp.where(c < (key + 1) * STRIDE, 1, 0) for c in codes)
        under = sum(jnp.where(c < key * STRIDE, 1, 0) for c in codes)
        last[key] = jnp.where(upto > under, upto, 0)
        return carry

    lax.fori_loop(0, key_count, ends, 0)


def kernel(
    sky_size, scale,
    pixels_in, cotangent_in, filters_in, target, source, live, chosen, tiles_in,
    outputs_out, pixel_grad_out, filter_grad_out,
    pixels, cotangent, filters, outputs, pixel_grad, filter_grad,
    tiles, ext0, ext1, ext2, latest, out_f0, out_f1, out_f2, out_b0, out_b1, out_b2,
    in_b0, in_b1, in_b2, cot_t, u, adj_three, adj_two, adj_one, adj_zero,
    part_f, part_b, part_a, grads,
    red_send_a, red_land_a, red_out_a, red_slots_a, red_final_a,
    red_send_b, red_land_b, red_out_b, red_slots_b, red_final_b,
    perm_f, perm_b, perm_a, keep_f, keep_b, keep_a, last_f, last_b, last_a,
    in_sem, out_sem, f_send, f_recv, b_send, b_recv, r_send, r_recv,
):
    me = lax.axis_index("sky")
    view = lax.axis_index("view")
    blocks, size, channels = pixels.shape
    max_tiles = tiles.shape[0]
    ext_count = ext0.shape[0]
    sends = (ext_count - blocks) // len(OFFSETS)
    radices = radices_of(sky_size)
    exts, outs_f = (ext0, ext1, ext2), (out_f0, out_f1, out_f2)
    outs_b, ins_b = (out_b0, out_b1, out_b2), (in_b0, in_b1, in_b2)

    loads = [
        pltpu.make_async_copy(src, dst, in_sem.at[number])
        for number, (src, dst) in enumerate((
            (pixels_in, pixels),
            (cotangent_in, cotangent),
            (filters_in, filters),
            (pixels_in, ext0.at[pl.ds(0, blocks)]),
            (tiles_in, tiles),
        ))
    ]
    stores = [
        pltpu.make_async_copy(src, dst, out_sem.at[number])
        for number, (src, dst) in enumerate((
            (outputs, outputs_out), (filter_grad, filter_grad_out), (pixel_grad, pixel_grad_out)
        ))
    ]
    for load in loads:
        load.start()

    def inside(place):
        return jnp.logical_and(place >= 0, place < sky_size)

    groups = []
    below = 1
    for radix in radices:
        spot = lax.rem(lax.div(me, below), radix)
        groups.append((below, radix, spot))
        below *= radix

    def partner(group, shift):
        below, radix, spot = group
        return me + (lax.rem(spot + shift, radix) - spot) * below

    barrier = pltpu.get_barrier_semaphore()
    peers = 1
    for offset in OFFSETS:
        peers = peers + jnp.where(inside(me + offset), 1, 0)
        @pl.when(inside(me + offset))
        def _():
            pl.semaphore_signal(barrier, inc=1, device_id={"sky": me + offset}, device_id_type=MESH)
    for group in groups:
        for shift in range(1, group[1]):
            other = partner(group, shift)
            far = (other - me) * (other - me) > 4
            peers = peers + jnp.where(far, 1, 0)
            @pl.when(far)
            def _():
                pl.semaphore_signal(barrier, inc=1, device_id={"sky": other}, device_id_type=MESH)
    pl.semaphore_signal(barrier, inc=1, device_id={"view": 1 - view}, device_id_type=MESH)

    for number, offset in enumerate(OFFSETS):
        at = pl.ds(blocks + number * sends, sends)
        @pl.when(jnp.logical_not(inside(me - offset)))
        def _():
            for ext in exts:
                ext[at] = jnp.zeros((sends, size, channels), jnp.bfloat16)

        @pl.when(jnp.logical_not(inside(me + offset)))
        def _():
            for landed in ins_b:
                landed[pl.ds(number * sends, sends)] = jnp.zeros(
                    (sends, channels, size), jnp.bfloat16
                )

    def stage_forward(step, blocks_ref):
        for slot in range(len(OFFSETS) * sends):
            outs_f[step][slot] = blocks_ref[chosen[slot]]

    def copy_forward(step, number):
        return pltpu.make_async_remote_copy(
            src_ref=outs_f[step].at[pl.ds(number * sends, sends)],
            dst_ref=exts[step].at[pl.ds(blocks + number * sends, sends)],
            send_sem=f_send.at[step, number],
            recv_sem=f_recv.at[step, number],
            device_id={"sky": me + OFFSETS[number]},
            device_id_type=MESH,
        )

    def copy_backward(step, number):
        return pltpu.make_async_remote_copy(
            src_ref=outs_b[step].at[pl.ds(number * sends, sends)],
            dst_ref=ins_b[step].at[pl.ds(number * sends, sends)],
            send_sem=b_send.at[step, number],
            recv_sem=b_recv.at[step, number],
            device_id={"sky": me - OFFSETS[number]},
            device_id_type=MESH,
        )

    def start_all(copy, step, sign):
        for number in (3, 2, 1, 0):
            @pl.when(inside(me + sign * OFFSETS[number]))
            def _():
                copy(step, number).start()

    def wait_arrivals(copy, step, sign):
        for number in range(len(OFFSETS)):
            @pl.when(inside(me - sign * OFFSETS[number]))
            def _():
                copy(step, number).wait_recv()

    def wait_departures(copy, step, sign):
        for number in range(len(OFFSETS)):
            @pl.when(inside(me + sign * OFFSETS[number]))
            def _():
                copy(step, number).wait_send()

    loads[0].wait()
    stage_forward(0, pixels)
    pl.semaphore_wait(barrier, peers)
    start_all(copy_forward, 0, 1)

    part_f[0] = jnp.zeros(part_f.shape[1:], jnp.float32)
    part_b[0] = jnp.zeros(part_b.shape[1:], jnp.float32)
    part_a[0] = jnp.zeros(part_a.shape[1:], jnp.float32)
    count = live[0]
    live_target = [jnp.where(t < count, target[t], blocks) for t in range(max_tiles)]
    live_source = [jnp.where(t < count, source[t], ext_count) for t in range(max_tiles)]
    order_slots(live_source, ext_count, perm_b, keep_b, last_b)
    order_slots([chosen[t] for t in range(len(OFFSETS) * sends)], blocks, perm_a, keep_a, last_a)
    order_slots(live_target, blocks, perm_f, keep_f, last_f)

    loads[1].wait()
    for b in range(blocks):
        cot_t[:, b * size : (b + 1) * size] = (
            cotangent[b].astype(jnp.float32).T.astype(jnp.bfloat16)
        )

    group = GROUP if max_tiles % GROUP == 0 else 1

    def scan_tiles(product, perm, keep, part):
        def body(step, total):
            for inner in range(group):
                place = step * group + inner
                total = product(perm[place]) + keep[place] * total
                part[place + 1] = total
            return total

        lax.fori_loop(0, max_tiles // group, body, jnp.zeros(part.shape[1:], jnp.float32))

    def forward(step):
        def product(t):
            return jnp.dot(
                tiles[t], exts[step][source[t]], preferred_element_type=jnp.float32
            )

        scan_tiles(product, perm_f, keep_f, part_f)

    def transposed(step):
        def product(t):
            return jnp.dot(u[target[t]], tiles[t], preferred_element_type=jnp.float32)

        scan_tiles(product, perm_b, keep_b, part_b)
        for slot in range(ext_count - blocks):
            outs_b[step][slot] = part_b[last_b[blocks + slot]].astype(jnp.bfloat16)

    def add_arrivals(step):
        wait_arrivals(copy_backward, step, -1)
        if step < 2:
            start_all(copy_forward, step + 1, 1)
        total = jnp.zeros((channels, size), jnp.float32)
        for place in range(len(OFFSETS) * sends):
            total = ins_b[step][perm_a[place]].astype(jnp.float32) + keep_a[place] * total
            part_a[place + 1] = total

    def pulled(order, b):
        return jnp.dot(
            filters[order], cot_t[:, b * size : (b + 1) * size],
            preferred_element_type=jnp.float32,
        )

    def gradient(order, member):
        found = jnp.dot(
            cot_t[...], member.reshape(blocks * size, channels),
            preferred_element_type=jnp.float32,
        )
        grads[pl.ds(order * channels, channels)] = found

    reducers = (
        (0, 3, red_send_a, red_land_a, red_out_a, red_slots_a, red_final_a),
        (3, 4, red_send_b, red_land_b, red_out_b, red_slots_b, red_final_b),
    )
    per_batch = 2 + sum(radix - 1 for radix in radices)

    def half_of(batch):
        return (reducers[batch][1] - reducers[batch][0]) * channels // 2

    def view_copy(batch, src, dst, sem):
        return pltpu.make_async_remote_copy(
            src_ref=src, dst_ref=dst,
            send_sem=r_send.at[batch, sem], recv_sem=r_recv.at[batch, sem],
            device_id={"view": 1 - view}, device_id_type=MESH,
        )

    def halves_copy(batch):
        return view_copy(batch, reducers[batch][2], reducers[batch][3], 0)

    def final_copy(batch):
        half = half_of(batch)
        mine = reducers[batch][6].at[pl.ds(pl.multiple_of(view * half, 16), half)]
        return view_copy(batch, mine, mine, 1)

    def group_copy(batch, level, shift):
        sem = 2 + sum(radix - 1 for radix in radices[:level]) + shift - 1
        return pltpu.make_async_remote_copy(
            src_ref=reducers[batch][4].at[level],
            dst_ref=reducers[batch][5].at[level, groups[level][2]],
            send_sem=r_send.at[batch, sem], recv_sem=r_recv.at[batch, sem],
            device_id={"sky": partner(groups[level], shift)}, device_id_type=MESH,
        )

    def send_halves(batch):
        first, half = reducers[batch][0] * channels, half_of(batch)
        theirs = pl.multiple_of(first + (1 - view) * half, 16)
        reducers[batch][2][...] = grads[pl.ds(theirs, half)].astype(jnp.bfloat16)
        halves_copy(batch).start()

    def send_level(batch, level, total):
        rounded = total.astype(jnp.bfloat16)
        reducers[batch][4][level] = rounded
        reducers[batch][5][level, groups[level][2]] = rounded
        for shift in range(1, radices[level]):
            group_copy(batch, level, shift).start()

    def sum_level(batch, level):
        for shift in range(1, radices[level]):
            group_copy(batch, level, shift).wait_recv()
        total = reducers[batch][5][level, 0].astype(jnp.float32)
        for spot in range(1, radices[level]):
            total = total + reducers[batch][5][level, spot].astype(jnp.float32)
        return total

    def reduce_step(batch, step):
        if step == 0:
            send_halves(batch)
            return
        if step == 1:
            halves_copy(batch).wait_recv()
            first, half = reducers[batch][0] * channels, half_of(batch)
            mine = pl.multiple_of(first + view * half, 16)
            total = grads[pl.ds(mine, half)] + reducers[batch][3][...].astype(jnp.float32)
        elif step <= 1 + len(radices):
            total = sum_level(batch, step - 2)
        else:
            final_copy(batch).wait_recv()
            for order in range(reducers[batch][0], reducers[batch][1]):
                at = pl.ds((order - reducers[batch][0]) * channels, channels)
                filter_grad[order] = (reducers[batch][6][at] * scale).T
            return
        if step <= len(radices):
            send_level(batch, step - 1, total)
        else:
            half = half_of(batch)
            reducers[batch][6][pl.ds(pl.multiple_of(view * half, 16), half)] = total
            final_copy(batch).start()

    steps = 3 + len(radices)

    loads[2].wait()
    for b in range(blocks):
        value = pulled(3, b)
        adj_three[b] = value
        u[b] = value.astype(jnp.bfloat16)
    loads[4].wait()
    transposed(0)
    for b in range(blocks):
        adj_two[b] = pulled(2, b) + 2.0 * part_b[last_b[b]]

    loads[3].wait()
    wait_arrivals(copy_forward, 0, 1)
    start_all(copy_backward, 0, -1)
    forward(0)
    for b in range(blocks):
        value = part_f[last_f[b]].astype(jnp.bfloat16)
        ext1[b] = value
        latest[b] = value
    stage_forward(1, latest)
    gradient(0, pixels[...])
    gradient(1, ext1[pl.ds(0, blocks)])

    add_arrivals(0)
    for b in range(blocks):
        value = adj_two[b] + 2.0 * part_a[last_a[b]]
        adj_two[b] = value
        u[b] = value.astype(jnp.bfloat16)
    transposed(1)
    for b in range(blocks):
        adj_one[b] = pulled(1, b) + 2.0 * part_b[last_b[b]] - adj_three[b]

    wait_arrivals(copy_forward, 1, 1)
    start_all(copy_backward, 1, -1)
    forward(1)
    for b in range(blocks):
        value = 2.0 * part_f[last_f[b]] - pixels[b].astype(jnp.float32)
        ext2[b] = value.astype(jnp.bfloat16)
        latest[b] = value.astype(jnp.bfloat16)
    stage_forward(2, latest)
    gradient(2, ext2[pl.ds(0, blocks)])
    reduce_step(0, 0)

    add_arrivals(1)
    for b in range(blocks):
        value = adj_one[b] + 2.0 * part_a[last_a[b]]
        adj_one[b] = value
        u[b] = value.astype(jnp.bfloat16)
    transposed(2)
    reduce_step(0, 1)
    for b in range(blocks):
        adj_zero[b] = pulled(0, b) + part_b[last_b[b]] - adj_two[b]

    wait_arrivals(copy_forward, 2, 1)
    start_all(copy_backward, 2, -1)
    forward(2)
    for b in range(blocks):
        value = 2.0 * part_f[last_f[b]] - ext1[b].astype(jnp.float32)
        latest[b] = value.astype(jnp.bfloat16)
    gradient(3, latest[...])
    reduce_step(1, 0)
    reduce_step(0, 2)
    reduce_step(1, 1)

    weights = filters[...].reshape(filters.shape[0] * channels, channels)
    for b in range(blocks):
        joined = jnp.concatenate([pixels[b], ext1[b], ext2[b], latest[b]], axis=1)
        outputs[b] = jnp.dot(joined, weights, preferred_element_type=jnp.float32).astype(
            jnp.bfloat16
        )
    stores[0].start()
    for step in range(2, steps):
        if step > 2:
            reduce_step(0, step)
        reduce_step(1, step)
    stores[1].start()

    add_arrivals(2)
    for b in range(blocks):
        value = adj_zero[b] + part_a[last_a[b]]
        pixel_grad[b] = value.T.astype(jnp.bfloat16)
    stores[2].start()

    for step in range(3):
        wait_departures(copy_forward, step, 1)
        wait_departures(copy_backward, step, -1)
    for batch in range(2):
        halves_copy(batch).wait_send()
        for level in range(len(radices)):
            for shift in range(1, radices[level]):
                group_copy(batch, level, shift).wait_send()
        final_copy(batch).wait_send()
    for store in stores:
        store.wait()


def per_device(
    sky_size, view_size,
    pixels, cotangent, filters, lap_tiles, tile_target, tile_source, tile_count, send_blocks
):
    _, max_tiles, size, _ = lap_tiles.shape
    rows, channels = pixels.shape[1:]
    orders = filters.shape[0]
    blocks = rows // size
    slots = send_blocks.shape[1] * send_blocks.shape[2]
    ext_count = blocks + slots
    radices = radices_of(sky_size)
    bf, f32 = jnp.bfloat16, jnp.float32
    anywhere = pl.BlockSpec(memory_space=pl.ANY)
    smem = functools.partial(pl.BlockSpec, memory_space=pltpu.SMEM)

    def reducer(count):
        half = count * channels // 2
        return [
            pltpu.VMEM((half, channels), bf),
            pltpu.VMEM((half, channels), bf),
            pltpu.VMEM((len(radices), half, channels), bf),
            pltpu.VMEM((len(radices), max(radices), half, channels), bf),
            pltpu.VMEM((2 * half, channels), f32),
        ]

    sems = 2 + sum(radix - 1 for radix in radices)
    scratch = (
        [pltpu.VMEM((blocks, size, channels), bf)] * 2
        + [pltpu.VMEM((orders, channels, channels), bf)]
        + [pltpu.VMEM((blocks, size, channels), bf)] * 2
        + [pltpu.VMEM((orders, channels, channels), f32)]
        + [pltpu.VMEM((max_tiles, size, size), bf)]
        + [pltpu.VMEM((ext_count, size, channels), bf)] * 3
        + [pltpu.VMEM((blocks, size, channels), bf)]
        + [pltpu.VMEM((slots, size, channels), bf)] * 3
        + [pltpu.VMEM((slots, channels, size), bf)] * 6
        + [pltpu.VMEM((channels, rows), bf), pltpu.VMEM((blocks, channels, size), bf)]
        + [pltpu.VMEM((blocks, channels, size), f32)] * 4
        + [
            pltpu.VMEM((max_tiles + 1, size, channels), f32),
            pltpu.VMEM((max_tiles + 1, channels, size), f32),
            pltpu.VMEM((slots + 1, channels, size), f32),
            pltpu.VMEM((orders * channels, channels), f32),
        ]
        + reducer(3)
        + reducer(1)
        + [pltpu.SMEM((max_tiles,), jnp.int32)] * 2
        + [pltpu.SMEM((slots,), jnp.int32)]
        + [pltpu.SMEM((max_tiles,), f32)] * 2
        + [pltpu.SMEM((slots,), f32)]
        + [
            pltpu.SMEM((blocks,), jnp.int32),
            pltpu.SMEM((ext_count,), jnp.int32),
            pltpu.SMEM((blocks,), jnp.int32),
        ]
        + [pltpu.SemaphoreType.DMA((5,)), pltpu.SemaphoreType.DMA((3,))]
        + [pltpu.SemaphoreType.DMA((3, len(OFFSETS)))] * 4
        + [pltpu.SemaphoreType.DMA((2, sems))] * 2
    )
    scale = 1.0 / math.sqrt(view_size * sky_size * rows)
    flops = 2 * channels * (6 * max_tiles * size * size + 3 * orders * rows * channels)
    outputs, pixel_grad, filter_grad = pl.pallas_call(
        functools.partial(kernel, sky_size, scale),
        out_shape=(
            jax.ShapeDtypeStruct((blocks, size, channels), bf),
            jax.ShapeDtypeStruct((blocks, size, channels), bf),
            jax.ShapeDtypeStruct((orders, channels, channels), f32),
        ),
        in_specs=[anywhere] * 3 + [smem()] * 4 + [anywhere],
        out_specs=(anywhere,) * 3,
        scratch_shapes=scratch,
        cost_estimate=pl.CostEstimate(
            flops=flops, bytes_accessed=2 * max_tiles * size * size, transcendentals=0
        ),
        compiler_params=pltpu.CompilerParams(
            collective_id=0, has_side_effects=True, vmem_limit_bytes=60 * 1024 * 1024
        ),
    )(
        pixels.reshape(blocks, size, channels),
        cotangent.reshape(blocks, size, channels),
        filters,
        tile_target.reshape(max_tiles),
        tile_source.reshape(max_tiles),
        tile_count,
        send_blocks.reshape(slots),
        lap_tiles.reshape(max_tiles, size, size),
    )
    return (
        outputs.reshape(1, rows, channels),
        pixel_grad.reshape(1, rows, channels),
        filter_grad,
    )


def solution(mesh):
    return jax.shard_map(
        functools.partial(per_device, mesh.shape["sky"], mesh.shape["view"]),
        mesh=mesh,
        in_specs=(
            P("view", "sky", None),
            P("view", "sky", None),
            P(),
            P("sky", None, None, None),
            P("sky", None),
            P("sky", None),
            P("sky"),
            P("sky", None, None),
        ),
        out_specs=(P("view", "sky", None), P("view", "sky", None), P()),
        check_vma=False,
    )
```

```python
import functools
import math

import jax
import jax.numpy as jnp
from jax import lax
from jax.experimental import pallas as pl
from jax.experimental.pallas import tpu as pltpu
from jax.sharding import PartitionSpec as P

OFFSETS = (1, -1, 2, -2)
MESH = pl.DeviceIdType.MESH
STRIDE = 64
BIG = 1 << 20
GROUP = 8


def radices_of(size):
    found = []
    while size > 1:
        step = 4 if size % 4 == 0 else (2 if size % 2 == 0 else size)
        found.append(step)
        size //= step
    return found


def smallest(values):
    while len(values) > 1:
        paired = [jnp.minimum(a, b) for a, b in zip(values[::2], values[1::2])]
        values = paired + (values[-1:] if len(values) % 2 else [])
    return values[0]


def order_slots(keys, key_count, perm, keep, last):
    codes = [key * STRIDE + number for number, key in enumerate(keys)]

    def pick(place, carry):
        before, before_key = carry
        code = smallest([jnp.where(c > before, c, BIG) for c in codes])
        key = lax.div(code, STRIDE)
        perm[place] = code - key * STRIDE
        keep[place] = jnp.where(key == before_key, 1.0, 0.0).astype(jnp.float32)
        return code, key

    lax.fori_loop(0, len(keys), pick, (jnp.int32(-1), jnp.int32(-1)))

    def ends(key, carry):
        upto = sum(jnp.where(c < (key + 1) * STRIDE, 1, 0) for c in codes)
        under = sum(jnp.where(c < key * STRIDE, 1, 0) for c in codes)
        last[key] = jnp.where(upto > under, upto, 0)
        return carry

    lax.fori_loop(0, key_count, ends, 0)


def kernel(
    sky_size, scale,
    pixels_in, cotangent_in, filters_in, target_in, source_in, live, chosen, tiles_in,
    outputs, pixel_grad, filter_grad,
    target, source, pixels, cotangent, filters,
    tiles, ext0, ext1, ext2, latest, out_f0, out_f1, out_f2, out_b0, out_b1, out_b2,
    in_b0, in_b1, in_b2, cot_t, u, adj_three, adj_two, adj_one, adj_zero,
    part_f, part_b, part_a, grads,
    red_send_a, red_land_a, red_out_a, red_slots_a, red_final_a,
    red_send_b, red_land_b, red_out_b, red_slots_b, red_final_b,
    perm_f, perm_b, perm_a, keep_f, keep_b, keep_a, last_f, last_b, last_a,
    in_sem, f_send, f_recv, b_send, b_recv, r_send, r_recv,
):
    me = lax.axis_index("sky")
    view = lax.axis_index("view")
    blocks, size, channels = pixels.shape
    max_tiles = tiles.shape[0]
    ext_count = ext0.shape[0]
    sends = (ext_count - blocks) // len(OFFSETS)
    radices = radices_of(sky_size)
    exts, outs_f = (ext0, ext1, ext2), (out_f0, out_f1, out_f2)
    outs_b, ins_b = (out_b0, out_b1, out_b2), (in_b0, in_b1, in_b2)

    loads = [
        pltpu.make_async_copy(src, dst, in_sem.at[number])
        for number, (src, dst) in enumerate((
            (pixels_in, pixels),
            (cotangent_in, cotangent),
            (filters_in, filters),
            (pixels_in, ext0.at[pl.ds(0, blocks)]),
            (tiles_in, tiles),
            (target_in, target),
            (source_in, source),
        ))
    ]
    for load in loads:
        load.start()

    def inside(place):
        return jnp.logical_and(place >= 0, place < sky_size)

    groups = []
    below = 1
    for radix in radices:
        spot = lax.rem(lax.div(me, below), radix)
        groups.append((below, radix, spot))
        below *= radix

    def partner(group, shift):
        below, radix, spot = group
        return me + (lax.rem(spot + shift, radix) - spot) * below

    barrier = pltpu.get_barrier_semaphore()
    peers = 1
    for offset in OFFSETS:
        peers = peers + jnp.where(inside(me + offset), 1, 0)
        @pl.when(inside(me + offset))
        def _():
            pl.semaphore_signal(barrier, inc=1, device_id={"sky": me + offset}, device_id_type=MESH)
    for group in groups:
        for shift in range(1, group[1]):
            other = partner(group, shift)
            far = (other - me) * (other - me) > 4
            peers = peers + jnp.where(far, 1, 0)
            @pl.when(far)
            def _():
                pl.semaphore_signal(barrier, inc=1, device_id={"sky": other}, device_id_type=MESH)
    pl.semaphore_signal(barrier, inc=1, device_id={"view": 1 - view}, device_id_type=MESH)

    for number, offset in enumerate(OFFSETS):
        at = pl.ds(blocks + number * sends, sends)
        @pl.when(jnp.logical_not(inside(me - offset)))
        def _():
            for ext in exts:
                ext[at] = jnp.zeros((sends, size, channels), jnp.bfloat16)

        @pl.when(jnp.logical_not(inside(me + offset)))
        def _():
            for landed in ins_b:
                landed[pl.ds(number * sends, sends)] = jnp.zeros(
                    (sends,) + landed.shape[1:], jnp.bfloat16
                )

    def stage_forward(step, blocks_ref):
        for slot in range(len(OFFSETS) * sends):
            outs_f[step][slot] = blocks_ref[chosen[0, slot // sends, slot % sends]]

    def copy_forward(step, number):
        return pltpu.make_async_remote_copy(
            src_ref=outs_f[step].at[pl.ds(number * sends, sends)],
            dst_ref=exts[step].at[pl.ds(blocks + number * sends, sends)],
            send_sem=f_send.at[step, number],
            recv_sem=f_recv.at[step, number],
            device_id={"sky": me + OFFSETS[number]},
            device_id_type=MESH,
        )

    def copy_backward(step, number):
        return pltpu.make_async_remote_copy(
            src_ref=outs_b[step].at[pl.ds(number * sends, sends)],
            dst_ref=ins_b[step].at[pl.ds(number * sends, sends)],
            send_sem=b_send.at[step, number],
            recv_sem=b_recv.at[step, number],
            device_id={"sky": me - OFFSETS[number]},
            device_id_type=MESH,
        )

    def start_all(copy, step, sign):
        for number in (3, 2, 1, 0):
            @pl.when(inside(me + sign * OFFSETS[number]))
            def _():
                copy(step, number).start()

    def wait_arrivals(copy, step, sign):
        for number in range(len(OFFSETS)):
            @pl.when(inside(me - sign * OFFSETS[number]))
            def _():
                copy(step, number).wait_recv()

    def wait_departures(copy, step, sign):
        for number in range(len(OFFSETS)):
            @pl.when(inside(me + sign * OFFSETS[number]))
            def _():
                copy(step, number).wait_send()

    loads[0].wait()
    stage_forward(0, pixels)
    pl.semaphore_wait(barrier, peers)
    start_all(copy_forward, 0, 1)

    part_f[0] = jnp.zeros(part_f.shape[1:], jnp.float32)
    part_b[0] = jnp.zeros(part_b.shape[1:], jnp.float32)
    part_a[0] = jnp.zeros(part_a.shape[1:], jnp.float32)
    loads[5].wait()
    loads[6].wait()
    count = live[0]
    live_target = [jnp.where(t < count, target[t], blocks) for t in range(max_tiles)]
    live_source = [jnp.where(t < count, source[t], ext_count) for t in range(max_tiles)]
    order_slots(live_source, ext_count, perm_b, keep_b, last_b)
    order_slots(
        [chosen[0, t // sends, t % sends] for t in range(len(OFFSETS) * sends)],
        blocks, perm_a, keep_a, last_a,
    )
    order_slots(live_target, blocks, perm_f, keep_f, last_f)

    loads[1].wait()
    for b in range(blocks):
        cot_t[:, b * size : (b + 1) * size] = (
            cotangent[b].astype(jnp.float32).T.astype(jnp.bfloat16)
        )

    group = GROUP if max_tiles % GROUP == 0 else 1

    def scan_tiles(product, perm, keep, part):
        def body(step, total):
            for inner in range(group):
                place = step * group + inner
                total = product(perm[place]) + keep[place] * total
                part[place + 1] = total
            return total

        lax.fori_loop(0, max_tiles // group, body, jnp.zeros(part.shape[1:], jnp.float32))

    def forward(step):
        def product(t):
            return jnp.dot(
                tiles[t], exts[step][source[t]], preferred_element_type=jnp.float32
            )

        scan_tiles(product, perm_f, keep_f, part_f)

    def transposed(step):
        def product(t):
            return jnp.dot(u[target[t]], tiles[t], preferred_element_type=jnp.float32)

        scan_tiles(product, perm_b, keep_b, part_b)
        for slot in range(ext_count - blocks):
            value = part_b[last_b[blocks + slot]]
            outs_b[step][slot] = (value.T if step == 2 else value).astype(jnp.bfloat16)

    def add_arrivals(step):
        if step < 2:
            wait_departures(copy_backward, step, -1)
            start_all(copy_forward, step + 1, 1)
        wait_arrivals(copy_backward, step, -1)
        part = part_f if step == 2 else part_a
        total = jnp.zeros(part.shape[1:], jnp.float32)
        for place in range(len(OFFSETS) * sends):
            total = ins_b[step][perm_a[place]].astype(jnp.float32) + keep_a[place] * total
            part[place + 1] = total

    def pulled(order, b):
        return jnp.dot(
            filters[order], cot_t[:, b * size : (b + 1) * size],
            preferred_element_type=jnp.float32,
        )

    def gradient(order, member):
        found = jnp.dot(
            cot_t[...], member.reshape(blocks * size, channels),
            preferred_element_type=jnp.float32,
        )
        grads[pl.ds(order * channels, channels)] = found

    reducers = (
        (0, 3, red_send_a, red_land_a, red_out_a, red_slots_a, red_final_a),
        (3, 4, red_send_b, red_land_b, red_out_b, red_slots_b, red_final_b),
    )
    per_batch = 2 + sum(radix - 1 for radix in radices)

    def half_of(batch):
        return (reducers[batch][1] - reducers[batch][0]) * channels // 2

    def view_copy(batch, src, dst, sem):
        return pltpu.make_async_remote_copy(
            src_ref=src, dst_ref=dst,
            send_sem=r_send.at[batch, sem], recv_sem=r_recv.at[batch, sem],
            device_id={"view": 1 - view}, device_id_type=MESH,
        )

    def halves_copy(batch):
        return view_copy(batch, reducers[batch][2], reducers[batch][3], 0)

    def final_copy(batch):
        half = half_of(batch)
        mine = reducers[batch][6].at[pl.ds(pl.multiple_of(view * half, 16), half)]
        return view_copy(batch, mine, mine, 1)

    def group_copy(batch, level, shift):
        sem = 2 + sum(radix - 1 for radix in radices[:level]) + shift - 1
        return pltpu.make_async_remote_copy(
            src_ref=reducers[batch][4].at[level],
            dst_ref=reducers[batch][5].at[level, groups[level][2]],
            send_sem=r_send.at[batch, sem], recv_sem=r_recv.at[batch, sem],
            device_id={"sky": partner(groups[level], shift)}, device_id_type=MESH,
        )

    def send_halves(batch):
        first, half = reducers[batch][0] * channels, half_of(batch)
        theirs = pl.multiple_of(first + (1 - view) * half, 16)
        reducers[batch][2][...] = grads[pl.ds(theirs, half)].astype(jnp.bfloat16)
        halves_copy(batch).start()

    def send_level(batch, level, total):
        rounded = total.astype(jnp.bfloat16)
        reducers[batch][4][level] = rounded
        reducers[batch][5][level, groups[level][2]] = rounded
        for shift in range(1, radices[level]):
            group_copy(batch, level, shift).start()

    def sum_level(batch, level):
        for shift in range(1, radices[level]):
            group_copy(batch, level, shift).wait_recv()
        total = reducers[batch][5][level, 0].astype(jnp.float32)
        for spot in range(1, radices[level]):
            total = total + reducers[batch][5][level, spot].astype(jnp.float32)
        return total

    def reduce_step(batch, step):
        if step == 0:
            send_halves(batch)
            return
        if step == 1:
            halves_copy(batch).wait_recv()
            first, half = reducers[batch][0] * channels, half_of(batch)
            mine = pl.multiple_of(first + view * half, 16)
            total = grads[pl.ds(mine, half)] + reducers[batch][3][...].astype(jnp.float32)
        elif step <= 1 + len(radices):
            total = sum_level(batch, step - 2)
        else:
            final_copy(batch).wait_recv()
            for order in range(reducers[batch][0], reducers[batch][1]):
                at = pl.ds((order - reducers[batch][0]) * channels, channels)
                filter_grad[order] = (reducers[batch][6][at] * scale).T
            return
        if step <= len(radices):
            send_level(batch, step - 1, total)
        else:
            half = half_of(batch)
            reducers[batch][6][pl.ds(pl.multiple_of(view * half, 16), half)] = total
            final_copy(batch).start()

    steps = 3 + len(radices)

    loads[2].wait()
    for b in range(blocks):
        value = pulled(3, b)
        adj_three[b] = value
        u[b] = value.astype(jnp.bfloat16)
    loads[4].wait()
    transposed(0)
    for b in range(blocks):
        adj_two[b] = pulled(2, b) + 2.0 * part_b[last_b[b]]

    loads[3].wait()
    wait_departures(copy_forward, 0, 1)
    start_all(copy_backward, 0, -1)
    wait_arrivals(copy_forward, 0, 1)
    forward(0)
    for b in range(blocks):
        value = part_f[last_f[b]].astype(jnp.bfloat16)
        ext1[b] = value
        latest[b] = value
    stage_forward(1, latest)
    gradient(0, pixels[...])
    gradient(1, ext1[pl.ds(0, blocks)])

    add_arrivals(0)
    for b in range(blocks):
        value = adj_two[b] + 2.0 * part_a[last_a[b]]
        adj_two[b] = value
        u[b] = value.astype(jnp.bfloat16)
    transposed(1)
    for b in range(blocks):
        adj_one[b] = pulled(1, b) + 2.0 * part_b[last_b[b]] - adj_three[b]

    wait_departures(copy_forward, 1, 1)
    start_all(copy_backward, 1, -1)
    wait_arrivals(copy_forward, 1, 1)
    forward(1)
    for b in range(blocks):
        value = 2.0 * part_f[last_f[b]] - pixels[b].astype(jnp.float32)
        ext2[b] = value.astype(jnp.bfloat16)
        latest[b] = value.astype(jnp.bfloat16)
    stage_forward(2, latest)
    gradient(2, ext2[pl.ds(0, blocks)])
    reduce_step(0, 0)

    add_arrivals(1)
    for b in range(blocks):
        value = adj_one[b] + 2.0 * part_a[last_a[b]]
        adj_one[b] = value
        u[b] = value.astype(jnp.bfloat16)
    transposed(2)
    reduce_step(0, 1)
    for b in range(blocks):
        adj_zero[b] = (pulled(0, b) + part_b[last_b[b]] - adj_two[b]).T

    wait_departures(copy_forward, 2, 1)
    start_all(copy_backward, 2, -1)
    wait_arrivals(copy_forward, 2, 1)
    forward(2)
    for b in range(blocks):
        value = 2.0 * part_f[last_f[b]] - ext1[b].astype(jnp.float32)
        latest[b] = value.astype(jnp.bfloat16)
    gradient(3, latest[...])
    reduce_step(1, 0)
    reduce_step(0, 2)
    reduce_step(1, 1)

    weights = filters[...].reshape(filters.shape[0] * channels, channels)
    for b in range(blocks):
        joined = jnp.concatenate([pixels[b], ext1[b], ext2[b], latest[b]], axis=1)
        outputs[b] = jnp.dot(joined, weights, preferred_element_type=jnp.float32).astype(
            jnp.bfloat16
        )
    for step in range(2, steps):
        if step > 2:
            reduce_step(0, step)
        reduce_step(1, step)

    add_arrivals(2)
    for b in range(blocks):
        pixel_grad[b] = (adj_zero[b] + part_f[last_a[b]]).astype(jnp.bfloat16)

    wait_departures(copy_backward, 2, -1)
    for batch in range(2):
        halves_copy(batch).wait_send()
        for level in range(len(radices)):
            for shift in range(1, radices[level]):
                group_copy(batch, level, shift).wait_send()
        final_copy(batch).wait_send()


def in_hbm(array):
    return pltpu.with_memory_space_constraint(array, pltpu.HBM)


def per_device(
    sky_size, view_size,
    pixels, cotangent, filters, lap_tiles, tile_target, tile_source, tile_count, send_blocks
):
    _, max_tiles, size, _ = lap_tiles.shape
    rows, channels = pixels.shape[1:]
    orders = filters.shape[0]
    blocks = rows // size
    slots = send_blocks.shape[1] * send_blocks.shape[2]
    ext_count = blocks + slots
    radices = radices_of(sky_size)
    bf, f32 = jnp.bfloat16, jnp.float32
    outside = pl.BlockSpec(memory_space=pltpu.HBM)
    smem = functools.partial(pl.BlockSpec, memory_space=pltpu.SMEM)

    def reducer(count):
        half = count * channels // 2
        return [
            pltpu.VMEM((half, channels), bf),
            pltpu.VMEM((half, channels), bf),
            pltpu.VMEM((len(radices), half, channels), bf),
            pltpu.VMEM((len(radices), max(radices), half, channels), bf),
            pltpu.VMEM((2 * half, channels), f32),
        ]

    sems = 2 + sum(radix - 1 for radix in radices)
    scratch = (
        [pltpu.SMEM((max_tiles,), jnp.int32)] * 2
        + [pltpu.VMEM((blocks, size, channels), bf)] * 2
        + [pltpu.VMEM((orders, channels, channels), bf)]
        + [pltpu.VMEM((max_tiles, size, size), bf)]
        + [pltpu.VMEM((ext_count, size, channels), bf)] * 3
        + [pltpu.VMEM((blocks, size, channels), bf)]
        + [pltpu.VMEM((slots, size, channels), bf)] * 3
        + [pltpu.VMEM((slots, channels, size), bf)] * 2
        + [pltpu.VMEM((slots, size, channels), bf)]
        + [pltpu.VMEM((slots, channels, size), bf)] * 2
        + [pltpu.VMEM((slots, size, channels), bf)]
        + [pltpu.VMEM((channels, rows), bf), pltpu.VMEM((blocks, channels, size), bf)]
        + [pltpu.VMEM((blocks, channels, size), f32)] * 3
        + [pltpu.VMEM((blocks, size, channels), f32)]
        + [
            pltpu.VMEM((max_tiles + 1, size, channels), f32),
            pltpu.VMEM((max_tiles + 1, channels, size), f32),
            pltpu.VMEM((slots + 1, channels, size), f32),
            pltpu.VMEM((orders * channels, channels), f32),
        ]
        + reducer(3)
        + reducer(1)
        + [pltpu.SMEM((max_tiles,), jnp.int32)] * 2
        + [pltpu.SMEM((slots,), jnp.int32)]
        + [pltpu.SMEM((max_tiles,), f32)] * 2
        + [pltpu.SMEM((slots,), f32)]
        + [
            pltpu.SMEM((blocks,), jnp.int32),
            pltpu.SMEM((ext_count,), jnp.int32),
            pltpu.SMEM((blocks,), jnp.int32),
        ]
        + [pltpu.SemaphoreType.DMA((7,))]
        + [pltpu.SemaphoreType.DMA((3, len(OFFSETS)))] * 4
        + [pltpu.SemaphoreType.DMA((2, sems))] * 2
    )
    scale = 1.0 / math.sqrt(view_size * sky_size * rows)
    flops = 2 * channels * (6 * max_tiles * size * size + 3 * orders * rows * channels)
    outputs, pixel_grad, filter_grad = pl.pallas_call(
        functools.partial(kernel, sky_size, scale),
        out_shape=(
            jax.ShapeDtypeStruct((blocks, size, channels), bf),
            jax.ShapeDtypeStruct((blocks, size, channels), bf),
            jax.ShapeDtypeStruct((orders, channels, channels), f32),
        ),
        in_specs=[outside] * 5 + [smem()] * 2 + [outside],
        out_specs=(pl.BlockSpec(memory_space=pltpu.VMEM),) * 3,
        scratch_shapes=scratch,
        cost_estimate=pl.CostEstimate(
            flops=flops, bytes_accessed=2 * max_tiles * size * size, transcendentals=0
        ),
        compiler_params=pltpu.CompilerParams(
            collective_id=0, has_side_effects=True, vmem_limit_bytes=48 * 1024 * 1024
        ),
    )(
        in_hbm(pixels.reshape(blocks, size, channels)),
        in_hbm(cotangent.reshape(blocks, size, channels)),
        in_hbm(filters),
        in_hbm(tile_target.reshape(max_tiles)),
        in_hbm(tile_source.reshape(max_tiles)),
        tile_count,
        send_blocks,
        in_hbm(lap_tiles.reshape(max_tiles, size, size)),
    )
    return (
        outputs.reshape(1, rows, channels),
        pixel_grad.reshape(1, rows, channels),
        filter_grad,
    )


def solution(mesh):
    return jax.shard_map(
        functools.partial(per_device, mesh.shape["sky"], mesh.shape["view"]),
        mesh=mesh,
        in_specs=(
            P("view", "sky", None),
            P("view", "sky", None),
            P(),
            P("sky", None, None, None),
            P("sky", None),
            P("sky", None),
            P("sky"),
            P("sky", None, None),
        ),
        out_specs=(P("view", "sky", None), P("view", "sky", None), P()),
        check_vma=False,
    )
```

```python
import functools
import math

import jax
import jax.numpy as jnp
from jax import lax
from jax.experimental import pallas as pl
from jax.experimental.pallas import tpu as pltpu
from jax.sharding import PartitionSpec as P

OFFSETS = (1, -1, 2, -2)
MESH = pl.DeviceIdType.MESH
STRIDE = 64
BIG = 1 << 20
GROUP = 12


def radices_of(size):
    found = []
    while size > 1:
        step = 4 if size % 4 == 0 else (2 if size % 2 == 0 else size)
        found.append(step)
        size //= step
    return found


def smallest(values):
    while len(values) > 1:
        paired = [jnp.minimum(a, b) for a, b in zip(values[::2], values[1::2])]
        values = paired + (values[-1:] if len(values) % 2 else [])
    return values[0]


def order_slots(keys, key_count, perm, keep, last):
    codes = [key * STRIDE + number for number, key in enumerate(keys)]

    def pick(place, carry):
        before, before_key = carry
        code = smallest([jnp.where(c > before, c, BIG) for c in codes])
        key = lax.div(code, STRIDE)
        perm[place] = code - key * STRIDE
        keep[place] = jnp.where(key == before_key, 1.0, 0.0).astype(jnp.float32)
        return code, key

    lax.fori_loop(0, len(keys), pick, (jnp.int32(-1), jnp.int32(-1)))

    def ends(key, carry):
        upto = sum(jnp.where(c < (key + 1) * STRIDE, 1, 0) for c in codes)
        under = sum(jnp.where(c < key * STRIDE, 1, 0) for c in codes)
        last[key] = jnp.where(upto > under, upto, 0)
        return carry

    lax.fori_loop(0, key_count, ends, 0)


def kernel(
    sky_size, scale,
    pixels_in, cotangent_in, filters_in, target_in, source_in, live, chosen, tiles_in,
    outputs, pixel_grad, filter_grad,
    target, source, pixels, cotangent, filters,
    tiles, ext0, ext1, ext2, latest, out_f0, out_f1, out_f2, out_b0, out_b1, out_b2,
    in_b0, in_b1, in_b2, cot_t, u, adj_three, adj_two, adj_one, adj_zero,
    part_f, part_b, part_a, grads,
    red_send_a, red_land_a, red_out_a, red_slots_a, red_final_a,
    red_send_b, red_land_b, red_out_b, red_slots_b, red_final_b,
    perm_f, perm_b, perm_a, keep_f, keep_b, keep_a, last_f, last_b, last_a,
    in_sem, f_send, f_recv, b_send, b_recv, r_send, r_recv,
):
    me = lax.axis_index("sky")
    view = lax.axis_index("view")
    blocks, size, channels = pixels.shape
    max_tiles = tiles.shape[0]
    ext_count = ext0.shape[0]
    sends = (ext_count - blocks) // len(OFFSETS)
    radices = radices_of(sky_size)
    exts, outs_f = (ext0, ext1, ext2), (out_f0, out_f1, out_f2)
    outs_b, ins_b = (out_b0, out_b1, out_b2), (in_b0, in_b1, in_b2)

    loads = [
        pltpu.make_async_copy(src, dst, in_sem.at[number])
        for number, (src, dst) in enumerate((
            (pixels_in, pixels),
            (cotangent_in, cotangent),
            (filters_in, filters),
            (pixels_in, ext0.at[pl.ds(0, blocks)]),
            (tiles_in, tiles),
            (target_in, target),
            (source_in, source),
        ))
    ]
    for load in loads:
        load.start()

    def inside(place):
        return jnp.logical_and(place >= 0, place < sky_size)

    groups = []
    below = 1
    for radix in radices:
        spot = lax.rem(lax.div(me, below), radix)
        groups.append((below, radix, spot))
        below *= radix

    def partner(group, shift):
        below, radix, spot = group
        return me + (lax.rem(spot + shift, radix) - spot) * below

    barrier = pltpu.get_barrier_semaphore()
    peers = 1
    for offset in OFFSETS:
        peers = peers + jnp.where(inside(me + offset), 1, 0)
        @pl.when(inside(me + offset))
        def _():
            pl.semaphore_signal(barrier, inc=1, device_id={"sky": me + offset}, device_id_type=MESH)
    for group in groups:
        for shift in range(1, group[1]):
            other = partner(group, shift)
            far = (other - me) * (other - me) > 4
            peers = peers + jnp.where(far, 1, 0)
            @pl.when(far)
            def _():
                pl.semaphore_signal(barrier, inc=1, device_id={"sky": other}, device_id_type=MESH)
    pl.semaphore_signal(barrier, inc=1, device_id={"view": 1 - view}, device_id_type=MESH)

    for number, offset in enumerate(OFFSETS):
        at = pl.ds(blocks + number * sends, sends)
        @pl.when(jnp.logical_not(inside(me - offset)))
        def _():
            for ext in exts:
                ext[at] = jnp.zeros((sends, size, channels), jnp.bfloat16)

        @pl.when(jnp.logical_not(inside(me + offset)))
        def _():
            for landed in ins_b:
                landed[pl.ds(number * sends, sends)] = jnp.zeros(
                    (sends,) + landed.shape[1:], jnp.bfloat16
                )

    def stage_forward(step, blocks_ref):
        for slot in range(len(OFFSETS) * sends):
            outs_f[step][slot] = blocks_ref[chosen[0, slot // sends, slot % sends]]

    def copy_forward(step, number):
        return pltpu.make_async_remote_copy(
            src_ref=outs_f[step].at[pl.ds(number * sends, sends)],
            dst_ref=exts[step].at[pl.ds(blocks + number * sends, sends)],
            send_sem=f_send.at[step, number],
            recv_sem=f_recv.at[step, number],
            device_id={"sky": me + OFFSETS[number]},
            device_id_type=MESH,
        )

    def copy_backward(step, number):
        return pltpu.make_async_remote_copy(
            src_ref=outs_b[step].at[pl.ds(number * sends, sends)],
            dst_ref=ins_b[step].at[pl.ds(number * sends, sends)],
            send_sem=b_send.at[step, number],
            recv_sem=b_recv.at[step, number],
            device_id={"sky": me - OFFSETS[number]},
            device_id_type=MESH,
        )

    def start_all(copy, step, sign):
        for number in (3, 2, 1, 0):
            @pl.when(inside(me + sign * OFFSETS[number]))
            def _():
                copy(step, number).start()

    def wait_arrivals(copy, step, sign):
        for number in range(len(OFFSETS)):
            @pl.when(inside(me - sign * OFFSETS[number]))
            def _():
                copy(step, number).wait_recv()

    def hand_over(done, done_step, sign, copy, step):
        for number in (3, 2, 1, 0):
            @pl.when(inside(me + sign * OFFSETS[number]))
            def _():
                done(done_step, number).wait_send()
                copy(step, number ^ 1).start()

    def wait_departures(copy, step, sign):
        for number in range(len(OFFSETS)):
            @pl.when(inside(me + sign * OFFSETS[number]))
            def _():
                copy(step, number).wait_send()

    loads[0].wait()
    stage_forward(0, pixels)
    pl.semaphore_wait(barrier, peers)
    start_all(copy_forward, 0, 1)

    part_f[0] = jnp.zeros(part_f.shape[1:], jnp.float32)
    part_b[0] = jnp.zeros(part_b.shape[1:], jnp.float32)
    part_a[0] = jnp.zeros(part_a.shape[1:], jnp.float32)
    loads[5].wait()
    loads[6].wait()
    count = live[0]
    live_target = [jnp.where(t < count, target[t], blocks) for t in range(max_tiles)]
    live_source = [jnp.where(t < count, source[t], ext_count) for t in range(max_tiles)]
    order_slots(live_source, ext_count, perm_b, keep_b, last_b)
    order_slots(
        [chosen[0, t // sends, t % sends] for t in range(len(OFFSETS) * sends)],
        blocks, perm_a, keep_a, last_a,
    )
    order_slots(live_target, blocks, perm_f, keep_f, last_f)

    loads[1].wait()
    for b in range(blocks):
        cot_t[:, b * size : (b + 1) * size] = (
            cotangent[b].astype(jnp.float32).T.astype(jnp.bfloat16)
        )

    group = GROUP if max_tiles % GROUP == 0 else 1

    def scan_tiles(product, perm, keep, part):
        def body(step, total):
            for inner in range(group):
                place = step * group + inner
                total = product(perm[place]) + keep[place] * total
                part[place + 1] = total
            return total

        lax.fori_loop(0, max_tiles // group, body, jnp.zeros(part.shape[1:], jnp.float32))

    def forward(step):
        def product(t):
            return jnp.dot(
                tiles[t], exts[step][source[t]], preferred_element_type=jnp.float32
            )

        scan_tiles(product, perm_f, keep_f, part_f)

    def transposed(step):
        def product(t):
            return jnp.dot(u[target[t]], tiles[t], preferred_element_type=jnp.float32)

        scan_tiles(product, perm_b, keep_b, part_b)
        for slot in range(ext_count - blocks):
            value = part_b[last_b[blocks + slot]]
            outs_b[step][slot] = (value.T if step == 2 else value).astype(jnp.bfloat16)

    def add_arrivals(step):
        if step < 2:
            hand_over(copy_backward, step, -1, copy_forward, step + 1)
        wait_arrivals(copy_backward, step, -1)
        part = part_f if step == 2 else part_a
        total = jnp.zeros(part.shape[1:], jnp.float32)
        for place in range(len(OFFSETS) * sends):
            total = ins_b[step][perm_a[place]].astype(jnp.float32) + keep_a[place] * total
            part[place + 1] = total

    def pulled(order, b):
        return jnp.dot(
            filters[order], cot_t[:, b * size : (b + 1) * size],
            preferred_element_type=jnp.float32,
        )

    def gradient(order, member):
        found = jnp.dot(
            cot_t[...], member.reshape(blocks * size, channels),
            preferred_element_type=jnp.float32,
        )
        grads[pl.ds(order * channels, channels)] = found

    reducers = (
        (0, 3, red_send_a, red_land_a, red_out_a, red_slots_a, red_final_a),
        (3, 4, red_send_b, red_land_b, red_out_b, red_slots_b, red_final_b),
    )
    per_batch = 2 + sum(radix - 1 for radix in radices)

    def half_of(batch):
        return (reducers[batch][1] - reducers[batch][0]) * channels // 2

    def view_copy(batch, src, dst, sem):
        return pltpu.make_async_remote_copy(
            src_ref=src, dst_ref=dst,
            send_sem=r_send.at[batch, sem], recv_sem=r_recv.at[batch, sem],
            device_id={"view": 1 - view}, device_id_type=MESH,
        )

    def halves_copy(batch):
        return view_copy(batch, reducers[batch][2], reducers[batch][3], 0)

    def final_copy(batch):
        half = half_of(batch)
        mine = reducers[batch][6].at[pl.ds(pl.multiple_of(view * half, 16), half)]
        return view_copy(batch, mine, mine, 1)

    def group_copy(batch, level, shift):
        sem = 2 + sum(radix - 1 for radix in radices[:level]) + shift - 1
        return pltpu.make_async_remote_copy(
            src_ref=reducers[batch][4].at[level],
            dst_ref=reducers[batch][5].at[level, groups[level][2]],
            send_sem=r_send.at[batch, sem], recv_sem=r_recv.at[batch, sem],
            device_id={"sky": partner(groups[level], shift)}, device_id_type=MESH,
        )

    def send_halves(batch):
        first, half = reducers[batch][0] * channels, half_of(batch)
        theirs = pl.multiple_of(first + (1 - view) * half, 16)
        reducers[batch][2][...] = grads[pl.ds(theirs, half)].astype(jnp.bfloat16)
        halves_copy(batch).start()

    def send_level(batch, level, total):
        rounded = total.astype(jnp.bfloat16)
        reducers[batch][4][level] = rounded
        reducers[batch][5][level, groups[level][2]] = rounded
        for shift in range(1, radices[level]):
            group_copy(batch, level, shift).start()

    def sum_level(batch, level):
        for shift in range(1, radices[level]):
            group_copy(batch, level, shift).wait_recv()
        total = reducers[batch][5][level, 0].astype(jnp.float32)
        for spot in range(1, radices[level]):
            total = total + reducers[batch][5][level, spot].astype(jnp.float32)
        return total

    def reduce_step(batch, step):
        if step == 0:
            send_halves(batch)
            return
        if step == 1:
            halves_copy(batch).wait_recv()
            first, half = reducers[batch][0] * channels, half_of(batch)
            mine = pl.multiple_of(first + view * half, 16)
            total = grads[pl.ds(mine, half)] + reducers[batch][3][...].astype(jnp.float32)
        elif step <= 1 + len(radices):
            total = sum_level(batch, step - 2)
        else:
            final_copy(batch).wait_recv()
            for order in range(reducers[batch][0], reducers[batch][1]):
                at = pl.ds((order - reducers[batch][0]) * channels, channels)
                filter_grad[order] = (reducers[batch][6][at] * scale).T
            return
        if step <= len(radices):
            send_level(batch, step - 1, total)
        else:
            half = half_of(batch)
            reducers[batch][6][pl.ds(pl.multiple_of(view * half, 16), half)] = total
            final_copy(batch).start()

    steps = 3 + len(radices)

    loads[2].wait()
    for b in range(blocks):
        value = pulled(3, b)
        adj_three[b] = value
        u[b] = value.astype(jnp.bfloat16)
    loads[4].wait()
    transposed(0)
    for b in range(blocks):
        adj_two[b] = pulled(2, b) + 2.0 * part_b[last_b[b]]

    loads[3].wait()
    hand_over(copy_forward, 0, 1, copy_backward, 0)
    wait_arrivals(copy_forward, 0, 1)
    forward(0)
    for b in range(blocks):
        value = part_f[last_f[b]].astype(jnp.bfloat16)
        ext1[b] = value
        latest[b] = value
    stage_forward(1, latest)
    gradient(0, pixels[...])
    gradient(1, ext1[pl.ds(0, blocks)])

    add_arrivals(0)
    for b in range(blocks):
        value = adj_two[b] + 2.0 * part_a[last_a[b]]
        adj_two[b] = value
        u[b] = value.astype(jnp.bfloat16)
    transposed(1)
    for b in range(blocks):
        adj_one[b] = pulled(1, b) + 2.0 * part_b[last_b[b]] - adj_three[b]

    hand_over(copy_forward, 1, 1, copy_backward, 1)
    wait_arrivals(copy_forward, 1, 1)
    forward(1)
    for b in range(blocks):
        value = 2.0 * part_f[last_f[b]] - pixels[b].astype(jnp.float32)
        ext2[b] = value.astype(jnp.bfloat16)
        latest[b] = value.astype(jnp.bfloat16)
    stage_forward(2, latest)
    gradient(2, ext2[pl.ds(0, blocks)])
    reduce_step(0, 0)

    add_arrivals(1)
    for b in range(blocks):
        value = adj_one[b] + 2.0 * part_a[last_a[b]]
        adj_one[b] = value
        u[b] = value.astype(jnp.bfloat16)
    transposed(2)
    reduce_step(0, 1)
    for b in range(blocks):
        adj_zero[b] = (pulled(0, b) + part_b[last_b[b]] - adj_two[b]).T

    hand_over(copy_forward, 2, 1, copy_backward, 2)
    wait_arrivals(copy_forward, 2, 1)
    forward(2)
    for b in range(blocks):
        value = 2.0 * part_f[last_f[b]] - ext1[b].astype(jnp.float32)
        latest[b] = value.astype(jnp.bfloat16)
    gradient(3, latest[...])
    reduce_step(1, 0)
    reduce_step(0, 2)
    reduce_step(1, 1)

    weights = filters[...].reshape(filters.shape[0] * channels, channels)
    for b in range(blocks):
        joined = jnp.concatenate([pixels[b], ext1[b], ext2[b], latest[b]], axis=1)
        outputs[b] = jnp.dot(joined, weights, preferred_element_type=jnp.float32).astype(
            jnp.bfloat16
        )
    for step in range(2, steps):
        if step > 2:
            reduce_step(0, step)
        reduce_step(1, step)

    add_arrivals(2)
    for b in range(blocks):
        pixel_grad[b] = (adj_zero[b] + part_f[last_a[b]]).astype(jnp.bfloat16)

    wait_departures(copy_backward, 2, -1)
    for batch in range(2):
        halves_copy(batch).wait_send()
        for level in range(len(radices)):
            for shift in range(1, radices[level]):
                group_copy(batch, level, shift).wait_send()
        final_copy(batch).wait_send()


def in_hbm(array):
    return pltpu.with_memory_space_constraint(array, pltpu.HBM)


def per_device(
    sky_size, view_size,
    pixels, cotangent, filters, lap_tiles, tile_target, tile_source, tile_count, send_blocks
):
    _, max_tiles, size, _ = lap_tiles.shape
    rows, channels = pixels.shape[1:]
    orders = filters.shape[0]
    blocks = rows // size
    slots = send_blocks.shape[1] * send_blocks.shape[2]
    ext_count = blocks + slots
    radices = radices_of(sky_size)
    bf, f32 = jnp.bfloat16, jnp.float32
    outside = pl.BlockSpec(memory_space=pltpu.HBM)
    smem = functools.partial(pl.BlockSpec, memory_space=pltpu.SMEM)

    def reducer(count):
        half = count * channels // 2
        return [
            pltpu.VMEM((half, channels), bf),
            pltpu.VMEM((half, channels), bf),
            pltpu.VMEM((len(radices), half, channels), bf),
            pltpu.VMEM((len(radices), max(radices), half, channels), bf),
            pltpu.VMEM((2 * half, channels), f32),
        ]

    sems = 2 + sum(radix - 1 for radix in radices)
    scratch = (
        [pltpu.SMEM((max_tiles,), jnp.int32)] * 2
        + [pltpu.VMEM((blocks, size, channels), bf)] * 2
        + [pltpu.VMEM((orders, channels, channels), bf)]
        + [pltpu.VMEM((max_tiles, size, size), bf)]
        + [pltpu.VMEM((ext_count, size, channels), bf)] * 3
        + [pltpu.VMEM((blocks, size, channels), bf)]
        + [pltpu.VMEM((slots, size, channels), bf)] * 3
        + [pltpu.VMEM((slots, channels, size), bf)] * 2
        + [pltpu.VMEM((slots, size, channels), bf)]
        + [pltpu.VMEM((slots, channels, size), bf)] * 2
        + [pltpu.VMEM((slots, size, channels), bf)]
        + [pltpu.VMEM((channels, rows), bf), pltpu.VMEM((blocks, channels, size), bf)]
        + [pltpu.VMEM((blocks, channels, size), f32)] * 3
        + [pltpu.VMEM((blocks, size, channels), f32)]
        + [
            pltpu.VMEM((max_tiles + 1, size, channels), f32),
            pltpu.VMEM((max_tiles + 1, channels, size), f32),
            pltpu.VMEM((slots + 1, channels, size), f32),
            pltpu.VMEM((orders * channels, channels), f32),
        ]
        + reducer(3)
        + reducer(1)
        + [pltpu.SMEM((max_tiles,), jnp.int32)] * 2
        + [pltpu.SMEM((slots,), jnp.int32)]
        + [pltpu.SMEM((max_tiles,), f32)] * 2
        + [pltpu.SMEM((slots,), f32)]
        + [
            pltpu.SMEM((blocks,), jnp.int32),
            pltpu.SMEM((ext_count,), jnp.int32),
            pltpu.SMEM((blocks,), jnp.int32),
        ]
        + [pltpu.SemaphoreType.DMA((7,))]
        + [pltpu.SemaphoreType.DMA((3, len(OFFSETS)))] * 4
        + [pltpu.SemaphoreType.DMA((2, sems))] * 2
    )
    scale = 1.0 / math.sqrt(view_size * sky_size * rows)
    flops = 2 * channels * (6 * max_tiles * size * size + 3 * orders * rows * channels)
    outputs, pixel_grad, filter_grad = pl.pallas_call(
        functools.partial(kernel, sky_size, scale),
        out_shape=(
            jax.ShapeDtypeStruct((blocks, size, channels), bf),
            jax.ShapeDtypeStruct((blocks, size, channels), bf),
            jax.ShapeDtypeStruct((orders, channels, channels), f32),
        ),
        in_specs=[outside] * 5 + [smem()] * 2 + [outside],
        out_specs=(pl.BlockSpec(memory_space=pltpu.VMEM),) * 3,
        scratch_shapes=scratch,
        cost_estimate=pl.CostEstimate(
            flops=flops, bytes_accessed=2 * max_tiles * size * size, transcendentals=0
        ),
        compiler_params=pltpu.CompilerParams(
            collective_id=0, has_side_effects=True, vmem_limit_bytes=48 * 1024 * 1024
        ),
    )(
        in_hbm(pixels.reshape(blocks, size, channels)),
        in_hbm(cotangent.reshape(blocks, size, channels)),
        in_hbm(filters),
        in_hbm(tile_target.reshape(max_tiles)),
        in_hbm(tile_source.reshape(max_tiles)),
        tile_count,
        send_blocks,
        in_hbm(lap_tiles.reshape(max_tiles, size, size)),
    )
    return (
        outputs.reshape(1, rows, channels),
        pixel_grad.reshape(1, rows, channels),
        filter_grad,
    )


def solution(mesh):
    return jax.shard_map(
        functools.partial(per_device, mesh.shape["sky"], mesh.shape["view"]),
        mesh=mesh,
        in_specs=(
            P("view", "sky", None),
            P("view", "sky", None),
            P(),
            P("sky", None, None, None),
            P("sky", None),
            P("sky", None),
            P("sky"),
            P("sky", None, None),
        ),
        out_specs=(P("view", "sky", None), P("view", "sky", None), P()),
        check_vma=False,
    )
```

```python
import functools
import math

import jax
import jax.numpy as jnp
from jax import lax
from jax.experimental import pallas as pl
from jax.experimental.pallas import tpu as pltpu
from jax.sharding import PartitionSpec as P

OFFSETS = (1, -1, 2, -2)
MESH = pl.DeviceIdType.MESH
STRIDE = 64
BIG = 1 << 20
GROUP = 12


def radices_of(size):
    found = []
    while size > 1:
        step = 4 if size % 4 == 0 else (2 if size % 2 == 0 else size)
        found.append(step)
        size //= step
    return found


def smallest(values):
    while len(values) > 1:
        paired = [jnp.minimum(a, b) for a, b in zip(values[::2], values[1::2])]
        values = paired + (values[-1:] if len(values) % 2 else [])
    return values[0]


def order_slots(keys, key_count, perm, keep, last):
    codes = [key * STRIDE + number for number, key in enumerate(keys)]

    def pick(place, carry):
        before, before_key = carry
        code = smallest([jnp.where(c > before, c, BIG) for c in codes])
        key = lax.div(code, STRIDE)
        perm[place] = code - key * STRIDE
        keep[place] = jnp.where(key == before_key, 1.0, 0.0).astype(jnp.float32)
        return code, key

    lax.fori_loop(0, len(keys), pick, (jnp.int32(-1), jnp.int32(-1)))

    def ends(key, carry):
        upto = sum(jnp.where(c < (key + 1) * STRIDE, 1, 0) for c in codes)
        under = sum(jnp.where(c < key * STRIDE, 1, 0) for c in codes)
        last[key] = jnp.where(upto > under, upto, 0)
        return carry

    lax.fori_loop(0, key_count, ends, 0)


def kernel(
    sky_size, scale,
    pixels_in, cotangent_in, filters_in, target_in, source_in, live, chosen, tiles_in,
    outputs, pixel_grad, filter_grad,
    target, source, pixels, cotangent, filters,
    tiles, ext0, ext1, ext2, latest, out_f0, out_f1, out_f2, out_b0, out_b1, out_b2,
    in_b0, in_b1, in_b2, cot_t, u, adj_three, adj_two, adj_one, adj_zero,
    part_f, part_b, part_a, grads,
    red_send_a, red_land_a, red_out_a, red_slots_a, red_final_a,
    red_send_b, red_land_b, red_out_b, red_slots_b, red_final_b,
    perm_f, perm_b, perm_a, keep_f, keep_b, keep_a, last_f, last_b, last_a,
    in_sem, f_send, f_recv, b_send, b_recv, r_send, r_recv,
):
    me = lax.axis_index("sky")
    view = lax.axis_index("view")
    blocks, size, channels = pixels.shape
    max_tiles = tiles.shape[0]
    ext_count = ext0.shape[0]
    sends = (ext_count - blocks) // len(OFFSETS)
    radices = radices_of(sky_size)
    exts, outs_f = (ext0, ext1, ext2), (out_f0, out_f1, out_f2)
    outs_b, ins_b = (out_b0, out_b1, out_b2), (in_b0, in_b1, in_b2)

    loads = [
        pltpu.make_async_copy(src, dst, in_sem.at[number])
        for number, (src, dst) in enumerate((
            (pixels_in, pixels),
            (cotangent_in, cotangent),
            (filters_in, filters),
            (pixels_in, ext0.at[pl.ds(0, blocks)]),
            (tiles_in, tiles),
            (target_in, target),
            (source_in, source),
        ))
    ]
    for load in loads:
        load.start()

    def inside(place):
        return jnp.logical_and(place >= 0, place < sky_size)

    groups = []
    below = 1
    for radix in radices:
        spot = lax.rem(lax.div(me, below), radix)
        groups.append((below, radix, spot))
        below *= radix

    def partner(group, shift):
        below, radix, spot = group
        return me + (lax.rem(spot + shift, radix) - spot) * below

    barrier = pltpu.get_barrier_semaphore()
    peers = 1
    for offset in OFFSETS:
        peers = peers + jnp.where(inside(me + offset), 1, 0)
        @pl.when(inside(me + offset))
        def _():
            pl.semaphore_signal(barrier, inc=1, device_id={"sky": me + offset}, device_id_type=MESH)
    for group in groups:
        for shift in range(1, group[1]):
            other = partner(group, shift)
            far = (other - me) * (other - me) > 4
            peers = peers + jnp.where(far, 1, 0)
            @pl.when(far)
            def _():
                pl.semaphore_signal(barrier, inc=1, device_id={"sky": other}, device_id_type=MESH)
    pl.semaphore_signal(barrier, inc=1, device_id={"view": 1 - view}, device_id_type=MESH)

    for number, offset in enumerate(OFFSETS):
        at = pl.ds(blocks + number * sends, sends)
        @pl.when(jnp.logical_not(inside(me - offset)))
        def _():
            for ext in exts:
                ext[at] = jnp.zeros((sends, size, channels), jnp.bfloat16)

        @pl.when(jnp.logical_not(inside(me + offset)))
        def _():
            for landed in ins_b:
                landed[pl.ds(number * sends, sends)] = jnp.zeros(
                    (sends,) + landed.shape[1:], jnp.bfloat16
                )

    def stage_forward(step, blocks_ref):
        for slot in range(len(OFFSETS) * sends):
            outs_f[step][slot] = blocks_ref[chosen[0, slot // sends, slot % sends]]

    def copy_forward(step, number):
        return pltpu.make_async_remote_copy(
            src_ref=outs_f[step].at[pl.ds(number * sends, sends)],
            dst_ref=exts[step].at[pl.ds(blocks + number * sends, sends)],
            send_sem=f_send.at[step, number],
            recv_sem=f_recv.at[step, number],
            device_id={"sky": me + OFFSETS[number]},
            device_id_type=MESH,
        )

    def copy_backward(step, number):
        return pltpu.make_async_remote_copy(
            src_ref=outs_b[step].at[pl.ds(number * sends, sends)],
            dst_ref=ins_b[step].at[pl.ds(number * sends, sends)],
            send_sem=b_send.at[step, number],
            recv_sem=b_recv.at[step, number],
            device_id={"sky": me - OFFSETS[number]},
            device_id_type=MESH,
        )

    def start_all(copy, step, sign):
        for number in (3, 2, 1, 0):
            @pl.when(inside(me + sign * OFFSETS[number]))
            def _():
                copy(step, number).start()

    def wait_arrivals(copy, step, sign):
        for number in range(len(OFFSETS)):
            @pl.when(inside(me - sign * OFFSETS[number]))
            def _():
                copy(step, number).wait_recv()

    def hand_over(done, done_step, sign, copy, step):
        for number in (3, 2, 1, 0):
            @pl.when(inside(me + sign * OFFSETS[number]))
            def _():
                done(done_step, number).wait_send()
                copy(step, number ^ 1).start()

    def wait_departures(copy, step, sign):
        for number in range(len(OFFSETS)):
            @pl.when(inside(me + sign * OFFSETS[number]))
            def _():
                copy(step, number).wait_send()

    loads[0].wait()
    stage_forward(0, pixels)
    pl.semaphore_wait(barrier, peers)
    start_all(copy_forward, 0, 1)

    part_f[0] = jnp.zeros(part_f.shape[1:], jnp.float32)
    part_b[0] = jnp.zeros(part_b.shape[1:], jnp.float32)
    part_a[0] = jnp.zeros(part_a.shape[1:], jnp.float32)
    loads[5].wait()
    loads[6].wait()
    count = live[0]
    live_target = [jnp.where(t < count, target[t], blocks) for t in range(max_tiles)]
    live_source = [jnp.where(t < count, source[t], ext_count) for t in range(max_tiles)]
    order_slots(live_source, ext_count, perm_b, keep_b, last_b)
    order_slots(
        [chosen[0, t // sends, t % sends] for t in range(len(OFFSETS) * sends)],
        blocks, perm_a, keep_a, last_a,
    )
    order_slots(live_target, blocks, perm_f, keep_f, last_f)

    loads[1].wait()
    for b in range(blocks):
        cot_t[:, b * size : (b + 1) * size] = (
            cotangent[b].astype(jnp.float32).T.astype(jnp.bfloat16)
        )

    group = GROUP if max_tiles % GROUP == 0 else 1

    def scan_tiles(product, perm, keep, part):
        def body(step, total):
            for inner in range(group):
                place = step * group + inner
                total = product(perm[place]) + keep[place] * total
                part[place + 1] = total
            return total

        lax.fori_loop(0, max_tiles // group, body, jnp.zeros(part.shape[1:], jnp.float32))

    def forward(step):
        def product(t):
            return jnp.dot(
                tiles[t], exts[step][source[t]], preferred_element_type=jnp.float32
            )

        scan_tiles(product, perm_f, keep_f, part_f)

    def transposed(step):
        def product(t):
            return jnp.dot(u[target[t]], tiles[t], preferred_element_type=jnp.float32)

        scan_tiles(product, perm_b, keep_b, part_b)
        for slot in range(ext_count - blocks):
            value = part_b[last_b[blocks + slot]]
            outs_b[step][slot] = (value.T if step == 2 else value).astype(jnp.bfloat16)

    def add_arrivals(step):
        if step < 2:
            hand_over(copy_backward, step, -1, copy_forward, step + 1)
        wait_arrivals(copy_backward, step, -1)
        part = part_f if step == 2 else part_a
        total = jnp.zeros(part.shape[1:], jnp.float32)
        for place in range(len(OFFSETS) * sends):
            total = ins_b[step][perm_a[place]].astype(jnp.float32) + keep_a[place] * total
            part[place + 1] = total

    def pulled(order, b):
        return jnp.dot(
            filters[order], cot_t[:, b * size : (b + 1) * size],
            preferred_element_type=jnp.float32,
        )

    def gradient(order, member):
        found = jnp.dot(
            cot_t[...], member.reshape(blocks * size, channels),
            preferred_element_type=jnp.float32,
        )
        grads[pl.ds(order * channels, channels)] = found

    reducers = (
        (0, 3, red_send_a, red_land_a, red_out_a, red_slots_a, red_final_a),
        (3, 4, red_send_b, red_land_b, red_out_b, red_slots_b, red_final_b),
    )
    per_batch = 2 + sum(radix - 1 for radix in radices)

    def half_of(batch):
        return (reducers[batch][1] - reducers[batch][0]) * channels // 2

    def view_copy(batch, src, dst, sem):
        return pltpu.make_async_remote_copy(
            src_ref=src, dst_ref=dst,
            send_sem=r_send.at[batch, sem], recv_sem=r_recv.at[batch, sem],
            device_id={"view": 1 - view}, device_id_type=MESH,
        )

    def halves_copy(batch):
        return view_copy(batch, reducers[batch][2], reducers[batch][3], 0)

    def final_copy(batch):
        half = half_of(batch)
        mine = reducers[batch][6].at[pl.ds(pl.multiple_of(view * half, 16), half)]
        return view_copy(batch, mine, mine, 1)

    def group_copy(batch, level, shift):
        sem = 2 + sum(radix - 1 for radix in radices[:level]) + shift - 1
        return pltpu.make_async_remote_copy(
            src_ref=reducers[batch][4].at[level],
            dst_ref=reducers[batch][5].at[level, groups[level][2]],
            send_sem=r_send.at[batch, sem], recv_sem=r_recv.at[batch, sem],
            device_id={"sky": partner(groups[level], shift)}, device_id_type=MESH,
        )

    def send_halves(batch):
        first, half = reducers[batch][0] * channels, half_of(batch)
        theirs = pl.multiple_of(first + (1 - view) * half, 16)
        reducers[batch][2][...] = grads[pl.ds(theirs, half)].astype(jnp.bfloat16)
        halves_copy(batch).start()

    def send_level(batch, level, total):
        rounded = total.astype(jnp.bfloat16)
        reducers[batch][4][level] = rounded
        reducers[batch][5][level, groups[level][2]] = rounded
        for shift in range(1, radices[level]):
            group_copy(batch, level, shift).start()

    def sum_level(batch, level):
        for shift in range(1, radices[level]):
            group_copy(batch, level, shift).wait_recv()
        total = reducers[batch][5][level, 0].astype(jnp.float32)
        for spot in range(1, radices[level]):
            total = total + reducers[batch][5][level, spot].astype(jnp.float32)
        return total

    def reduce_step(batch, step):
        if step == 0:
            send_halves(batch)
            return
        if step == 1:
            halves_copy(batch).wait_recv()
            first, half = reducers[batch][0] * channels, half_of(batch)
            mine = pl.multiple_of(first + view * half, 16)
            total = grads[pl.ds(mine, half)] + reducers[batch][3][...].astype(jnp.float32)
        elif step <= 1 + len(radices):
            total = sum_level(batch, step - 2)
        else:
            final_copy(batch).wait_recv()
            for order in range(reducers[batch][0], reducers[batch][1]):
                at = pl.ds((order - reducers[batch][0]) * channels, channels)
                filter_grad[order] = (reducers[batch][6][at] * scale).T
            return
        if step <= len(radices):
            send_level(batch, step - 1, total)
        else:
            half = half_of(batch)
            reducers[batch][6][pl.ds(pl.multiple_of(view * half, 16), half)] = total
            final_copy(batch).start()

    steps = 3 + len(radices)

    loads[2].wait()
    for b in range(blocks):
        value = pulled(3, b)
        adj_three[b] = value
        u[b] = value.astype(jnp.bfloat16)
    loads[4].wait()
    transposed(0)
    for b in range(blocks):
        adj_two[b] = pulled(2, b) + 2.0 * part_b[last_b[b]]

    loads[3].wait()
    hand_over(copy_forward, 0, 1, copy_backward, 0)
    wait_arrivals(copy_forward, 0, 1)
    forward(0)
    for b in range(blocks):
        value = part_f[last_f[b]].astype(jnp.bfloat16)
        ext1[b] = value
        latest[b] = value
    stage_forward(1, latest)
    gradient(0, pixels[...])
    gradient(1, ext1[pl.ds(0, blocks)])

    add_arrivals(0)
    for b in range(blocks):
        value = adj_two[b] + 2.0 * part_a[last_a[b]]
        adj_two[b] = value
        u[b] = value.astype(jnp.bfloat16)
    transposed(1)
    for b in range(blocks):
        adj_one[b] = pulled(1, b) + 2.0 * part_b[last_b[b]] - adj_three[b]

    hand_over(copy_forward, 1, 1, copy_backward, 1)
    wait_arrivals(copy_forward, 1, 1)
    forward(1)
    for b in range(blocks):
        value = 2.0 * part_f[last_f[b]] - pixels[b].astype(jnp.float32)
        ext2[b] = value.astype(jnp.bfloat16)
        latest[b] = value.astype(jnp.bfloat16)
    stage_forward(2, latest)
    gradient(2, ext2[pl.ds(0, blocks)])
    reduce_step(0, 0)

    add_arrivals(1)
    for b in range(blocks):
        value = adj_one[b] + 2.0 * part_a[last_a[b]]
        adj_one[b] = value
        u[b] = value.astype(jnp.bfloat16)
    transposed(2)
    reduce_step(0, 1)
    for b in range(blocks):
        adj_zero[b] = (pulled(0, b) + part_b[last_b[b]] - adj_two[b]).T

    hand_over(copy_forward, 2, 1, copy_backward, 2)
    wait_arrivals(copy_forward, 2, 1)
    forward(2)
    for b in range(blocks):
        value = 2.0 * part_f[last_f[b]] - ext1[b].astype(jnp.float32)
        latest[b] = value.astype(jnp.bfloat16)
    gradient(3, latest[...])
    reduce_step(1, 0)
    reduce_step(0, 2)
    reduce_step(1, 1)

    weights = filters[...].reshape(filters.shape[0] * channels, channels)
    for b in range(blocks):
        joined = jnp.concatenate([pixels[b], ext1[b], ext2[b], latest[b]], axis=1)
        outputs[b] = jnp.dot(joined, weights, preferred_element_type=jnp.float32).astype(
            jnp.bfloat16
        )
    for step in range(2, steps - 1):
        if step > 2:
            reduce_step(0, step)
        reduce_step(1, step)
    reduce_step(0, steps - 1)

    add_arrivals(2)
    for b in range(blocks):
        pixel_grad[b] = (adj_zero[b] + part_f[last_a[b]]).astype(jnp.bfloat16)
    reduce_step(1, steps - 1)

    wait_departures(copy_backward, 2, -1)
    for batch in range(2):
        halves_copy(batch).wait_send()
        for level in range(len(radices)):
            for shift in range(1, radices[level]):
                group_copy(batch, level, shift).wait_send()
        final_copy(batch).wait_send()


def in_hbm(array):
    return pltpu.with_memory_space_constraint(array, pltpu.HBM)


def per_device(
    sky_size, view_size,
    pixels, cotangent, filters, lap_tiles, tile_target, tile_source, tile_count, send_blocks
):
    _, max_tiles, size, _ = lap_tiles.shape
    rows, channels = pixels.shape[1:]
    orders = filters.shape[0]
    blocks = rows // size
    slots = send_blocks.shape[1] * send_blocks.shape[2]
    ext_count = blocks + slots
    radices = radices_of(sky_size)
    bf, f32 = jnp.bfloat16, jnp.float32
    outside = pl.BlockSpec(memory_space=pltpu.HBM)
    smem = functools.partial(pl.BlockSpec, memory_space=pltpu.SMEM)

    def reducer(count):
        half = count * channels // 2
        return [
            pltpu.VMEM((half, channels), bf),
            pltpu.VMEM((half, channels), bf),
            pltpu.VMEM((len(radices), half, channels), bf),
            pltpu.VMEM((len(radices), max(radices), half, channels), bf),
            pltpu.VMEM((2 * half, channels), f32),
        ]

    sems = 2 + sum(radix - 1 for radix in radices)
    scratch = (
        [pltpu.SMEM((max_tiles,), jnp.int32)] * 2
        + [pltpu.VMEM((blocks, size, channels), bf)] * 2
        + [pltpu.VMEM((orders, channels, channels), bf)]
        + [pltpu.VMEM((max_tiles, size, size), bf)]
        + [pltpu.VMEM((ext_count, size, channels), bf)] * 3
        + [pltpu.VMEM((blocks, size, channels), bf)]
        + [pltpu.VMEM((slots, size, channels), bf)] * 3
        + [pltpu.VMEM((slots, channels, size), bf)] * 2
        + [pltpu.VMEM((slots, size, channels), bf)]
        + [pltpu.VMEM((slots, channels, size), bf)] * 2
        + [pltpu.VMEM((slots, size, channels), bf)]
        + [pltpu.VMEM((channels, rows), bf), pltpu.VMEM((blocks, channels, size), bf)]
        + [pltpu.VMEM((blocks, channels, size), f32)] * 3
        + [pltpu.VMEM((blocks, size, channels), f32)]
        + [
            pltpu.VMEM((max_tiles + 1, size, channels), f32),
            pltpu.VMEM((max_tiles + 1, channels, size), f32),
            pltpu.VMEM((slots + 1, channels, size), f32),
            pltpu.VMEM((orders * channels, channels), f32),
        ]
        + reducer(3)
        + reducer(1)
        + [pltpu.SMEM((max_tiles,), jnp.int32)] * 2
        + [pltpu.SMEM((slots,), jnp.int32)]
        + [pltpu.SMEM((max_tiles,), f32)] * 2
        + [pltpu.SMEM((slots,), f32)]
        + [
            pltpu.SMEM((blocks,), jnp.int32),
            pltpu.SMEM((ext_count,), jnp.int32),
            pltpu.SMEM((blocks,), jnp.int32),
        ]
        + [pltpu.SemaphoreType.DMA((7,))]
        + [pltpu.SemaphoreType.DMA((3, len(OFFSETS)))] * 4
        + [pltpu.SemaphoreType.DMA((2, sems))] * 2
    )
    scale = 1.0 / math.sqrt(view_size * sky_size * rows)
    flops = 2 * channels * (6 * max_tiles * size * size + 3 * orders * rows * channels)
    outputs, pixel_grad, filter_grad = pl.pallas_call(
        functools.partial(kernel, sky_size, scale),
        out_shape=(
            jax.ShapeDtypeStruct((blocks, size, channels), bf),
            jax.ShapeDtypeStruct((blocks, size, channels), bf),
            jax.ShapeDtypeStruct((orders, channels, channels), f32),
        ),
        in_specs=[outside] * 5 + [smem()] * 2 + [outside],
        out_specs=(pl.BlockSpec(memory_space=pltpu.VMEM),) * 3,
        scratch_shapes=scratch,
        cost_estimate=pl.CostEstimate(
            flops=flops, bytes_accessed=2 * max_tiles * size * size, transcendentals=0
        ),
        compiler_params=pltpu.CompilerParams(
            collective_id=0, has_side_effects=True, vmem_limit_bytes=48 * 1024 * 1024
        ),
    )(
        in_hbm(pixels.reshape(blocks, size, channels)),
        in_hbm(cotangent.reshape(blocks, size, channels)),
        in_hbm(filters),
        in_hbm(tile_target.reshape(max_tiles)),
        in_hbm(tile_source.reshape(max_tiles)),
        tile_count,
        send_blocks,
        in_hbm(lap_tiles.reshape(max_tiles, size, size)),
    )
    return (
        outputs.reshape(1, rows, channels),
        pixel_grad.reshape(1, rows, channels),
        filter_grad,
    )


def solution(mesh):
    return jax.shard_map(
        functools.partial(per_device, mesh.shape["sky"], mesh.shape["view"]),
        mesh=mesh,
        in_specs=(
            P("view", "sky", None),
            P("view", "sky", None),
            P(),
            P("sky", None, None, None),
            P("sky", None),
            P("sky", None),
            P("sky"),
            P("sky", None, None),
        ),
        out_specs=(P("view", "sky", None), P("view", "sky", None), P()),
        check_vma=False,
    )
```
